256 devices in a mesh: gz: 32 (over y, z), gy: 8 (over x, core).
Axes of the slice: x: 4, y: 4, z: 8, core: 2. Of those that a mesh axis runs over, the one named last changes fastest.
Arguments:
- fraction: float32 [256, 256, 512], P('gz', 'gy'), may hold values from 0 to 1
- source: float32 [256, 256, 512], P('gz', 'gy'), may hold values from -40 to 40, as said below
- bubble_label: int32 [256, 256, 512], P('gz', 'gy'), may hold values from -1 to 4095, as said below
- subdomain: int32 [256, 256, 512], P('gz', 'gy'), may hold values from 0 to 1023, as said below
- coarse_inverse: float32 [5120, 5120], P(('gz', 'gy')), may hold values from -0.2 to 0.2, as said below
Outputs:
- iterate: float32 [256, 256, 512], P('gz', 'gy')
- residual: float32 [256, 256, 512], P('gz', 'gy')
The draws below stay inside these ranges and needn't reach their ends.
Inputs may be any that keep to these rules, and one draw needn't show every extreme that they name: `source`: vertical factor 1 + 2 z / 256, so magnitudes grow with depth. `bubble_label`: A cell at plane z and row y carries -1 or the number of a bubble of slab block a and row block y // 32 with |a - z // 8| <= 1; the bubbles of slab block a and row block b are numbered (a 8 + b) * 16 + i with i < 16. Rows y with y % 32 == 0 carry -1. `subdomain`: cells of slab block a and row block b carry (a 8 + b) * 4 + i with i < 4; the number does not change along z and y inside a block and never falls along x. `coarse_inverse`: symmetric positive definite.
All inputs are finite; a program needn't handle non-finite values.
Results may differ from the reference program's by a relative error of at most 0.0003.
Values sent between devices are 32-bit elements; how exact they have to be, the bound alone decides.
A program may use at most 64 MiB of HBM per device.

```python
from functools import reduce
import jax
import jax.numpy as jnp
from jax import lax

NX = 512
CZ = 8
CY = 32
S_DEV = 4
B_DEV = 16
ITERS = 3
NZ = 256
NY = 256
COARSE = 5120


def draw_source(key, part):
    noise = jnp.clip(jax.random.normal(key, (NZ, NY, NX), jnp.float32), -4.0, 4.0)
    depth = 1.0 + 2.0 * jnp.arange(NZ, dtype=jnp.float32)[:, None, None] / NZ
    return jnp.clip(3.0 * depth * noise, -40.0, 40.0)


def draw_bubble_label(key, part):
    slabs = NZ // CZ
    columns = NY // CY
    keys = jax.random.split(jax.random.fold_in(key, 11), 6)
    shape = (slabs, columns, B_DEV)
    radius_z = jax.random.randint(keys[0], shape, 1, CZ // 2 + 1)
    radius_y = jax.random.randint(keys[1], shape, 1, CY // 4 + 1)
    radius_x = jax.random.randint(keys[2], shape, 1, NX // 8 + 1)
    centre_z = jax.random.randint(keys[3], shape, 0, CZ)
    centre_y = radius_y + 1 + jax.random.randint(keys[4], shape, 0, CY - 2 * radius_y - 1)
    centre_x = jax.random.randint(keys[5], shape, 0, NX)
    local_z = jnp.arange(CZ, dtype=jnp.int32)[None, :, None, None]
    local_y = jnp.arange(CY, dtype=jnp.int32)[None, None, :, None]
    local_x = jnp.arange(NX, dtype=jnp.int32)[None, None, None, :]
    numbers = jnp.arange(B_DEV, dtype=jnp.int32)

    def block(index):
        slab = index // columns
        column = index % columns
        best = jnp.full((CZ, CY, NX), -1, jnp.int32)
        for offset in (-1, 0, 1):
            source_slab = jnp.clip(slab + offset, 0, slabs - 1)
            live = (slab + offset >= 0) & (slab + offset < slabs)
            middle_z = (source_slab * CZ + centre_z[source_slab, column] - slab * CZ)[:, None, None, None]
            inside = jnp.abs(local_z - middle_z) <= radius_z[source_slab, column][:, None, None, None]
            inside = inside & (jnp.abs(local_y - centre_y[source_slab, column][:, None, None, None]) <= radius_y[source_slab, column][:, None, None, None])
            inside = inside & (jnp.abs(local_x - centre_x[source_slab, column][:, None, None, None]) <= radius_x[source_slab, column][:, None, None, None])
            inside = inside & live
            ident = ((source_slab * columns + column) * B_DEV + numbers)[:, None, None, None]
            best = jnp.maximum(best, jnp.max(jnp.where(inside, ident, -1), axis=0))
        return best
    blocks = lax.map(block, jnp.arange(slabs * columns, dtype=jnp.int32))
    return blocks.reshape(slabs, columns, CZ, CY, NX).transpose(0, 2, 1, 3, 4).reshape(NZ, NY, NX).astype(jnp.int32)


def draw_subdomain(key, part):
    slabs = NZ // CZ
    columns = NY // CY
    cuts = jax.random.randint(jax.random.fold_in(key, 13), (slabs, columns, S_DEV - 1), 1, NX)
    across = jnp.arange(NX, dtype=jnp.int32)
    local = jnp.sum((across[None, None, :, None] >= cuts[:, :, None, :]).astype(jnp.int32), axis=-1)
    owner = jnp.arange(slabs, dtype=jnp.int32)[:, None, None] * columns + jnp.arange(columns, dtype=jnp.int32)[None, :, None]
    ident = owner * S_DEV + local
    full = jnp.broadcast_to(ident[:, None, :, None, :], (slabs, CZ, columns, CY, NX))
    return full.reshape(NZ, NY, NX).astype(jnp.int32)


def draw_coarse_inverse(key, part):
    first, second = jax.random.split(jax.random.fold_in(key, 17))
    span = S_DEV + B_DEV
    slot = jnp.arange(COARSE, dtype=jnp.int32) % span
    base = jnp.where(slot < S_DEV, 0.3 / jnp.sqrt(jnp.float32(CZ * CY * NX / S_DEV)), 0.3 / 8.0)
    spread = jnp.exp(jax.random.uniform(first, (COARSE,), jnp.float32, jnp.log(0.5), jnp.log(2.0)))
    scale = jnp.sqrt(base * spread)
    noise = jax.random.normal(second, (COARSE, COARSE), jnp.float32) * (0.35 / jnp.sqrt(2.0 * COARSE))
    rows = jnp.arange(COARSE, dtype=jnp.int32)
    same = rows[:, None] == rows[None, :]
    middle = jnp.where(same, 1.0, noise + noise.T)
    return (scale[:, None] * middle * scale[None, :]).astype(jnp.float32)


def block_scale(key, extent, pieces, smallest, largest):
    gain = 1.0
    for dim, shards_of in pieces:
        draws = jax.random.uniform(jax.random.fold_in(jax.random.fold_in(key, 6), dim), (shards_of,), jnp.float32, smallest / len(pieces), largest / len(pieces))
        gain = gain * jnp.repeat(jnp.exp(draws), extent[dim] // shards_of).reshape((-1,) + (1,) * (len(extent) - 1 - dim))
    return gain


def setup_inputs(seed: int = 0) -> dict:
    key_of = jax.random.split(jax.random.key(seed), 6)
    return {
        "fraction": jnp.clip(1.0 * jax.random.uniform(key_of[0], (NZ, NY, NX), jnp.float32) ** block_scale(key_of[0], (NZ, NY, NX), ((0, 32), (1, 8)), -0.2, 0.2), 0.0, 1.0),
        "source": draw_source(jax.random.fold_in(key_of[5], 71), 0),
        "bubble_label": draw_bubble_label(jax.random.fold_in(key_of[5], 71), 0),
        "subdomain": draw_subdomain(jax.random.fold_in(key_of[5], 71), 0),
        "coarse_inverse": draw_coarse_inverse(jax.random.fold_in(key_of[5], 71), 0),
    }


surface_tension = 0.5
shift_term = 0.05
gas_drop = 0.75
norm_floor = 0.25

def add_all(items):
    return reduce(lambda first, second: first + second, items)

def six_neighbours(padded):
    return [padded[2:, 1:-1, 1:-1], padded[:-2, 1:-1, 1:-1], padded[1:-1, 2:, 1:-1], padded[1:-1, :-2, 1:-1], padded[1:-1, 1:-1, 2:], padded[1:-1, 1:-1, :-2]]

def normals(padded):
    along = [0.5 * (padded[2:, 1:-1, 1:-1] - padded[:-2, 1:-1, 1:-1]), 0.5 * (padded[1:-1, 2:, 1:-1] - padded[1:-1, :-2, 1:-1]), 0.5 * (padded[1:-1, 1:-1, 2:] - padded[1:-1, 1:-1, :-2])]
    length = jnp.maximum(jnp.sqrt(along[0] * along[0] + along[1] * along[1] + along[2] * along[2]), norm_floor)
    return jnp.stack([member / length for member in along])

def curvature(padded):
    return -(0.5 * (padded[0, 2:, 1:-1, 1:-1] - padded[0, :-2, 1:-1, 1:-1]) + 0.5 * (padded[1, 1:-1, 2:, 1:-1] - padded[1, 1:-1, :-2, 1:-1]) + 0.5 * (padded[2, 1:-1, 1:-1, 2:] - padded[2, 1:-1, 1:-1, :-2]))

def assemble(frac_padded, kappa_padded, source):
    density = 1.0 - gas_drop * frac_padded
    centre = density[1:-1, 1:-1, 1:-1]
    coefs = [2.0 / (centre + other) for other in six_neighbours(density)]
    fraction = frac_padded[1:-1, 1:-1, 1:-1]
    kappa = kappa_padded[1:-1, 1:-1, 1:-1]
    terms = [coef * (0.5 * (kappa + kappa_other)) * (frac_other - fraction) for coef, frac_other, kappa_other in zip(coefs, six_neighbours(frac_padded), six_neighbours(kappa_padded))]
    rhs = source - surface_tension * add_all(terms)
    diagonal = shift_term + add_all(coefs)
    return (coefs, diagonal, rhs)

def operate_padded(padded, coefs, diagonal):
    return diagonal * padded[1:-1, 1:-1, 1:-1] - add_all([coef * other for coef, other in zip(coefs, six_neighbours(padded))])

def factor_planes(diagonal_planes, down_planes):
    inverse = [1.0 / diagonal_planes[0]]
    mults = [None]
    for level in range(1, len(diagonal_planes)):
        mult = down_planes[level] * inverse[level - 1]
        inverse.append(1.0 / (diagonal_planes[level] - mult * down_planes[level]))
        mults.append(mult)
    return (inverse, mults)

def solve_planes(values, inverse, mults, up_planes):
    count = len(values)
    forward = [values[0]]
    for level in range(1, count):
        forward.append(values[level] + mults[level] * forward[level - 1])
    result = [forward[count - 1] * inverse[count - 1]]
    for level in range(count - 2, -1, -1):
        result.insert(0, (forward[level] + up_planes[level] * result[0]) * inverse[level])
    return result

def reference(fraction, source, bubble_label, subdomain, coarse_inverse):
    frac_padded = jnp.pad(fraction, 1)
    normal = normals(frac_padded)
    kappa = curvature(jnp.pad(normal, ((0, 0), (1, 1), (1, 1), (1, 1))))
    kappa_padded = jnp.pad(kappa, 1)
    coefs, diagonal, rhs = assemble(frac_padded, kappa_padded, source)
    blocks = NZ // CZ

    def planes_of(field):
        shaped = field.reshape(blocks, CZ, NY, NX)
        return [shaped[:, level] for level in range(CZ)]

    def join(planes):
        return jnp.stack(planes, axis=1).reshape(NZ, NY, NX)
    inverse, mults = factor_planes(planes_of(diagonal), planes_of(coefs[1]))
    up_planes = planes_of(coefs[0])
    span = S_DEV + B_DEV
    column = jnp.where(bubble_label >= 0, bubble_label // B_DEV * span + S_DEV + bubble_label % B_DEV, subdomain // S_DEV * span + subdomain % S_DEV).astype(jnp.int32)
    flat_column = column.reshape(-1)

    def precondition(residual):
        block = join(solve_planes(planes_of(residual), inverse, mults, up_planes))
        totals = jax.ops.segment_sum(residual.reshape(-1), flat_column, num_segments=COARSE)
        coarse = jnp.dot(coarse_inverse, totals, precision=lax.Precision.HIGHEST)
        correction = jnp.take(coarse, flat_column).reshape(residual.shape)
        direction = block + correction
        return (direction, jnp.sum(residual * direction))

    def operate(field):
        return operate_padded(jnp.pad(field, 1), coefs, diagonal)
    iterate = jnp.zeros_like(rhs)
    residual = rhs
    direction, product = precondition(residual)
    search = direction
    for sweep in range(ITERS):
        image = operate(search)
        alpha = product / jnp.sum(search * image)
        iterate = iterate + alpha * search
        residual = residual - alpha * image
        if sweep + 1 < ITERS:
            direction, fresh = precondition(residual)
            search = direction + fresh / product * search
            product = fresh
    return (iterate, residual)
```

```python
import functools

import jax
import jax.numpy as jnp
from jax import lax
from jax.experimental import pallas as pl
from jax.experimental.pallas import tpu as pltpu
from jax.sharding import PartitionSpec as P

MESH = pl.DeviceIdType.MESH
CZ, CY, NX = 8, 32, 512
S_DEV, B_DEV = 4, 16
SPAN = S_DEV + B_DEV
SLABS, COLS = 32, 8
DEVS = SLABS * COLS
f32 = jnp.float32


def lanes_of(shape):
    return lax.broadcasted_iota(jnp.int32, shape, len(shape) - 1)


def x_plus(v):
    n = v.shape[-1]
    return jnp.where(lanes_of(v.shape) == n - 1, 0.0, pltpu.roll(v, n - 1, 1))


def x_minus(v):
    return jnp.where(lanes_of(v.shape) == 0, 0.0, pltpu.roll(v, 1, 1))


def far_first(n, half):
    return half + ((n + 1) // 2) * (1 - 2 * lax.rem(n, 2))


def kernel(
    frac, src, lab, sub, cinv, out_x, out_r,
    F, NRM, KAP, SRC, LB, SB, BN, CV, CW, CZF, CYP, CYM, CXP, CXM, DG, IV,
    R0, W, BL, Z, HBZ, HBY, HZ, HY, HBN, HYO, T2, X, YB, YS, M, G, M3, G3,
    ld, fs, fr, bsn, brc, cs, cr, ks, kr, gs, gr,
):
    a = lax.axis_index("gz")
    b = lax.axis_index("gy")
    me = b * SLABS + a
    here = a * COLS + b
    phys_y, phys_z, phys_x, core = a // 8, lax.rem(a, 8), b // 2, lax.rem(b, 2)
    up, down = lax.rem(a + 1, SLABS), lax.rem(a + SLABS - 1, SLABS)
    right, left = lax.rem(b + 1, COLS), lax.rem(b + COLS - 1, COLS)

    loads = [
        pltpu.make_async_copy(frac, F.at[pl.ds(3, CZ), pl.ds(16, CY)], ld.at[0]),
        pltpu.make_async_copy(src, SRC, ld.at[1]),
        pltpu.make_async_copy(lab, LB, ld.at[2]),
        pltpu.make_async_copy(sub, SB, ld.at[3]),
        pltpu.make_async_copy(cinv, CV, ld.at[4]),
    ]
    for copy in loads:
        copy.start()

    def partner(k):
        ty = lax.rem(phys_y + far_first(lax.rem(k // 8, 4), 2), 4)
        tz = lax.rem(phys_z + far_first(k // 32, 4), 8)
        tx = lax.rem(phys_x + far_first(lax.rem(k // 2, 4), 2), 4)
        tc = lax.rem(core + 1 - lax.rem(k, 2), 2)
        ta, tb = ty * 8 + tz, tx * 2 + tc
        return ta, tb

    bar = pltpu.get_barrier_semaphore()

    def greet(k, c):
        pl.semaphore_signal(bar, inc=1, device_id=partner(k), device_id_type=MESH)
        return c

    lax.fori_loop(0, DEVS - 1, greet, 0)
    pl.semaphore_wait(bar, DEVS - 1)

    def remote(source, target, send, recv, device):
        return pltpu.make_async_remote_copy(
            src_ref=source, dst_ref=target, send_sem=send, recv_sem=recv, device_id=device, device_id_type=MESH
        )

    halo = [
        remote(frac.at[pl.ds(0, 3)], F.at[pl.ds(11, 3), pl.ds(16, CY)], fs.at[0], fr.at[0], (down, b)),
        remote(frac.at[pl.ds(5, 3)], F.at[pl.ds(0, 3), pl.ds(16, CY)], fs.at[1], fr.at[1], (up, b)),
        remote(frac.at[:, pl.ds(24, 8)], F.at[pl.ds(3, CZ), pl.ds(8, 8)], fs.at[2], fr.at[2], (a, right)),
        remote(frac.at[:, pl.ds(0, 8)], F.at[pl.ds(3, CZ), pl.ds(48, 8)], fs.at[3], fr.at[3], (a, left)),
        remote(frac.at[pl.ds(6, 2), pl.ds(24, 8)], F.at[pl.ds(1, 2), pl.ds(8, 8)], fs.at[4], fr.at[4], (up, right)),
        remote(frac.at[pl.ds(6, 2), pl.ds(0, 8)], F.at[pl.ds(1, 2), pl.ds(48, 8)], fs.at[5], fr.at[5], (up, left)),
        remote(frac.at[pl.ds(0, 2), pl.ds(24, 8)], F.at[pl.ds(11, 2), pl.ds(8, 8)], fs.at[6], fr.at[6], (down, right)),
        remote(frac.at[pl.ds(0, 2), pl.ds(0, 8)], F.at[pl.ds(11, 2), pl.ds(48, 8)], fs.at[7], fr.at[7], (down, left)),
    ]
    for copy in halo:
        copy.start()

    loads[2].wait()
    loads[3].wait()

    def bins_plane(z, c):
        label, domain = LB[z], SB[z]
        off = (label >> 7) - a
        shift = jnp.where(off == 0, S_DEV, jnp.where(off < 0, SPAN, SPAN + B_DEV))
        BN[z] = jnp.where(label >= 0, (label & 15) + shift, domain - here * S_DEV)
        return c

    lax.fori_loop(0, CZ, bins_plane, 0)
    bins_out = [
        remote(BN.at[0], HBZ.at[1], bsn.at[0], brc.at[0], (down, b)),
        remote(BN.at[CZ - 1], HBZ.at[0], bsn.at[1], brc.at[1], (up, b)),
        remote(BN.at[:, pl.ds(24, 8)], HBY.at[0], bsn.at[2], brc.at[2], (a, right)),
        remote(BN.at[:, pl.ds(0, 8)], HBY.at[1], bsn.at[3], brc.at[3], (a, left)),
    ]
    for copy in bins_out:
        copy.start()

    loads[4].wait()
    first = CV[pl.ds(0, 8), :]
    CW[pl.ds(0, 8), :] = jnp.where(lax.broadcasted_iota(jnp.int32, first.shape, 0) < S_DEV, first, 0.0)
    CW[pl.ds(8, B_DEV), :] = CV[pl.ds(S_DEV, B_DEV), :]
    rows_out = [
        remote(CW.at[pl.ds(8, B_DEV)], CW.at[pl.ds(24, B_DEV)], cs.at[0], cr.at[0], (up, b)),
        remote(CW.at[pl.ds(8, B_DEV)], CW.at[pl.ds(40, B_DEV)], cs.at[1], cr.at[1], (down, b)),
    ]
    for copy in rows_out:
        copy.start()
    X[...] = jnp.zeros_like(X)
    YB[...] = jnp.zeros_like(YB)
    YS[...] = jnp.zeros_like(YS)
    T2[...] = jnp.zeros_like(T2)

    loads[0].wait()
    loads[1].wait()
    for copy in halo:
        copy.wait_recv()

    @pl.when(a == 0)
    def _():
        F[pl.ds(0, 3)] = jnp.zeros((3,) + F.shape[1:], f32)

    @pl.when(a == SLABS - 1)
    def _():
        F[pl.ds(11, 3)] = jnp.zeros((3,) + F.shape[1:], f32)

    @pl.when(b == 0)
    def _():
        F[:, pl.ds(8, 8)] = jnp.zeros((F.shape[0], 8, NX), f32)

    @pl.when(b == COLS - 1)
    def _():
        F[:, pl.ds(48, 8)] = jnp.zeros((F.shape[0], 8, NX), f32)

    def row_valid(first_row, shape):
        row = lax.broadcasted_iota(jnp.int32, shape, 0) + (first_row - 16 + b * CY)
        return (row >= 0) & (row < COLS * CY)

    def z_valid(z):
        place = a * CZ + z
        return (place >= 0) & (place < SLABS * CZ)

    wide = (8, 24, 40)

    def normals_plane(n, c):
        inside = z_valid(n - 2)
        for r in wide:
            rows = pl.ds(r, 16)
            centre = F[n + 1, rows, :]
            gz = 0.5 * (F[n + 2, rows, :] - F[n, rows, :])
            gy = 0.5 * (F[n + 1, pl.ds(r + 1, 16), :] - F[n + 1, pl.ds(r - 1, 16), :])
            gx = 0.5 * (x_plus(centre) - x_minus(centre))
            scale = jnp.minimum(lax.rsqrt(gz * gz + gy * gy + gx * gx), 4.0)
            scale = jnp.where(row_valid(r, scale.shape) & inside, scale, 0.0)
            NRM[0, n, rows, :] = gz * scale
            NRM[1, n, rows, :] = gy * scale
            NRM[2, n, rows, :] = gx * scale
        return c

    lax.fori_loop(0, CZ + 4, normals_plane, 0)

    def kappa_plane(n, c):
        inside = z_valid(n - 1)
        for r in wide:
            rows = pl.ds(r, 16)
            nx = NRM[2, n + 1, rows, :]
            value = -(
                0.5 * (NRM[0, n + 2, rows, :] - NRM[0, n, rows, :])
                + 0.5 * (NRM[1, n + 1, pl.ds(r + 1, 16), :] - NRM[1, n + 1, pl.ds(r - 1, 16), :])
                + 0.5 * (x_plus(nx) - x_minus(nx))
            )
            KAP[n, rows, :] = jnp.where(row_valid(r, value.shape) & inside, value, 0.0)
        return c

    lax.fori_loop(0, CZ + 2, kappa_plane, 0)

    def density(v):
        return 1.0 - 0.75 * v

    def faces_plane(n, c):
        for r in (0, 16):
            rows = pl.ds(16 + r, 16)
            CZF[n, pl.ds(r, 16), :] = 2.0 / (density(F[n + 2, rows, :]) + density(F[n + 3, rows, :]))
        return c

    lax.fori_loop(0, CZ + 1, faces_plane, 0)

    def assemble_plane(z, c):
        for r in range(0, CY, 8):
            rows, mine = pl.ds(16 + r, 8), pl.ds(r, 8)
            fc, kc = F[z + 3, rows, :], KAP[z + 1, rows, :]
            dc = density(fc)
            fy = (F[z + 3, pl.ds(17 + r, 8), :], F[z + 3, pl.ds(15 + r, 8), :])
            fx = (x_plus(fc), x_minus(fc))
            cz = (CZF[z + 1, mine, :], CZF[z, mine, :])
            cy = tuple(2.0 / (dc + density(v)) for v in fy)
            cx = tuple(2.0 / (dc + density(v)) for v in fx)
            CYP[z, mine, :], CYM[z, mine, :] = cy
            CXP[z, mine, :], CXM[z, mine, :] = cx
            DG[z, mine, :] = 0.05 + (cz[0] + cz[1] + cy[0] + cy[1] + cx[0] + cx[1])
            term = cz[0] * (0.5 * (kc + KAP[z + 2, rows, :])) * (F[z + 4, rows, :] - fc)
            term = term + cz[1] * (0.5 * (kc + KAP[z, rows, :])) * (F[z + 2, rows, :] - fc)
            term = term + cy[0] * (0.5 * (kc + KAP[z + 1, pl.ds(17 + r, 8), :])) * (fy[0] - fc)
            term = term + cy[1] * (0.5 * (kc + KAP[z + 1, pl.ds(15 + r, 8), :])) * (fy[1] - fc)
            term = term + cx[0] * (0.5 * (kc + x_plus(kc))) * (fx[0] - fc)
            term = term + cx[1] * (0.5 * (kc + x_minus(kc))) * (fx[1] - fc)
            R0[z, mine, :] = SRC[z, mine, :] - 0.5 * term
        return c

    lax.fori_loop(0, CZ, assemble_plane, 0)

    def factor_rows(i, c):
        rows = pl.ds(pl.multiple_of(i * 8, 8), 8)
        inverse = 1.0 / DG[0, rows, :]
        IV[0, rows, :] = inverse
        for z in range(1, CZ):
            face = CZF[z, rows, :]
            inverse = 1.0 / (DG[z, rows, :] - (face * inverse) * face)
            IV[z, rows, :] = inverse
        return c

    lanes_row = lanes_of((1, 128))

    def region_sums(v_ref):
        for group in range(3):
            base = S_DEV + B_DEV * group

            def tile(t, acc, base=base, group=group):
                z, rows = t // 4, pl.ds(pl.multiple_of(lax.rem(t, 4) * 8, 8), 8)
                bins, v = BN[z, rows, :], v_ref[z, rows, :]
                new = []
                for k in range(B_DEV):
                    picked = jnp.where(bins == base + k, v, 0.0)
                    new.append(
                        acc[k]
                        + ((picked[:, 0:128] + picked[:, 128:256]) + (picked[:, 256:384] + picked[:, 384:512]))
                    )
                return tuple(new)

            acc = lax.fori_loop(0, CZ * 4, tile, tuple(jnp.zeros((8, 128), f32) for _ in range(B_DEV)))
            for k in range(B_DEV):
                T2[pl.ds(8 + B_DEV * group + k, 1), :] = jnp.sum(acc[k], axis=0, keepdims=True)

        def liquid(t, acc):
            z, rows = t // 4, pl.ds(pl.multiple_of(lax.rem(t, 4) * 8, 8), 8)
            return acc + jnp.where(BN[z, rows, :] < S_DEV, v_ref[z, rows, :], 0.0)

        acc = lax.fori_loop(0, CZ * 4, liquid, jnp.zeros((8, NX), f32))
        domain = SB[0, pl.ds(0, 8), :] - here * S_DEV
        for k in range(S_DEV):
            picked = jnp.sum(jnp.where(domain == k, acc, 0.0), axis=0, keepdims=True)
            T2[pl.ds(k, 1), :] = (picked[:, 0:128] + picked[:, 128:256]) + (picked[:, 256:384] + picked[:, 384:512])
        return jnp.sum(T2[...], axis=1, keepdims=True)

    def exchange(k, sums, dots):
        for g in range(8):
            part = jnp.sum(CW[:, pl.ds(640 * g, 640)] * sums, axis=0, keepdims=True)
            for j in range(4):
                moved = part if j == 0 else pltpu.roll(part, 640 - 160 * j, 1)
                X[pl.ds(8 + 4 * g + j, 1), :] = moved[:, 0:256]
        wide_lanes = lanes_of((SLABS, 128))
        rows = pl.ds(8, SLABS)
        for t in range(COLS):
            if t <= 5:
                moved = X[rows, pl.ds(0, 128)]
                moved = moved if t == 0 else pltpu.roll(moved, 128 - SPAN * t, 1)
            elif t == 6:
                moved = pltpu.roll(X[rows, :], 256 - SPAN * t, 1)[:, 0:128]
            else:
                moved = pltpu.roll(X[rows, pl.ds(128, 128)], 256 - SPAN * t, 1)
            YS[t, rows, :] = jnp.where(wide_lanes < S_DEV, moved, 0.0)
            YB[t, rows, :] = jnp.where((wide_lanes >= S_DEV) & (wide_lanes < SPAN), moved, 0.0)
        before = None
        for t in range(COLS):
            row0 = (
                (YS[t, rows, :] + YB[t, rows, :])
                + pltpu.roll(YB[t, pl.ds(7, SLABS), :], 16, 1)
                + pltpu.roll(YB[t, pl.ds(9, SLABS), :], 32, 1)
                + pltpu.roll(YB[t, pl.ds(6, SLABS), :], 48, 1)
                + pltpu.roll(YB[t, pl.ds(10, SLABS), :], 64, 1)
                + pltpu.roll(YS[t, pl.ds(7, SLABS), :], 84, 1)
                + pltpu.roll(YS[t, pl.ds(9, SLABS), :], 88, 1)
            )
            if t + 1 < COLS:
                row0 = row0 + pltpu.roll(YS[t + 1, rows, :], 92, 1)
            row1 = jnp.broadcast_to(dots, (SLABS, 128))
            if before is not None:
                row1 = row1 + jnp.where(wide_lanes < SPAN + 2 * B_DEV, before, 0.0)
            M[k, pl.ds(SLABS * t, SLABS), 0, :] = row0
            M[k, pl.ds(SLABS * t, SLABS), 1, :] = row1
            before = row0

        def post(n, c):
            ta, tb = partner(n)
            remote(M.at[k, tb * SLABS + ta], G.at[k, me], gs.at[k], gr.at[k], (ta, tb)).start()
            return c

        lax.fori_loop(0, DEVS - 1, post, 0)
        G[k, me] = M[k, me]

    def collect(k):
        part = G.at[k, pl.ds(0, DEVS - 1)]
        pltpu.make_async_copy(part, part, gr.at[k]).wait()

        def add(i, acc):
            return acc + G[k, pl.ds(8 * i, 8)]

        total = jnp.sum(lax.fori_loop(0, DEVS // 8, add, jnp.zeros((8, 2, 128), f32)), axis=0)
        return total[0:1, :], total[1:2, :]

    def block_solve(v_ref, o_ref):
        def solve_rows(i, c):
            rows = pl.ds(pl.multiple_of(i * 8, 8), 8)
            inv = [IV[z, rows, :] for z in range(CZ)]
            face = [CZF[z, rows, :] for z in range(1, CZ)]
            held = [v_ref[0, rows, :] * inv[0]]
            for z in range(1, CZ):
                held.append((v_ref[z, rows, :] + face[z - 1] * held[z - 1]) * inv[z])
            value = held[CZ - 1]
            o_ref[CZ - 1, rows, :] = value
            for z in range(CZ - 2, -1, -1):
                value = held[z] + (face[z] * value) * inv[z]
                o_ref[z, rows, :] = value
            return c

        lax.fori_loop(0, CY // 8, solve_rows, 0)

    def send_block_halo(k):
        o_ref = BL.at[k]
        for z in range(CZ):
            HYO[k, 0, pl.ds(z, 1), :] = BL[k, z, pl.ds(CY - 1, 1), :]
            HYO[k, 1, pl.ds(z, 1), :] = BL[k, z, pl.ds(0, 1), :]
        out = [
            remote(o_ref.at[0], HZ.at[k, 1], ks.at[k, 0], kr.at[k, 0], (down, b)),
            remote(o_ref.at[CZ - 1], HZ.at[k, 0], ks.at[k, 1], kr.at[k, 1], (up, b)),
            remote(HYO.at[k, 0], HY.at[k, 0], ks.at[k, 2], kr.at[k, 2], (a, right)),
            remote(HYO.at[k, 1], HY.at[k, 1], ks.at[k, 3], kr.at[k, 3], (a, left)),
        ]
        for copy in out:
            copy.start()
        return out

    def pick(table, bins):
        rows = bins.shape[0]
        spread = jnp.broadcast_to(table, (rows, 128))
        return jnp.concatenate(
            [
                jnp.take_along_axis(spread, bins[:, 128 * i : 128 * i + 128], axis=1, mode="promise_in_bounds")
                for i in range(NX // 128)
            ],
            axis=1,
        )

    def combine(ref_at, coefs):
        value = ref_at(0)
        for i, coef in enumerate(coefs):
            value = value - coef * ref_at(i + 1)
        return value

    def total_of(acc):
        part = jnp.sum(acc, axis=0, keepdims=True)
        return jnp.sum(part, axis=1, keepdims=True)

    def direction(k, tables0, tables1, coefs, other):
        table0 = combine(lambda i: tables0[i], coefs)
        table1 = combine(lambda i: tables1[i], coefs)

        def plane(z, acc):
            rz, zs = acc
            for r in range(0, CY, 8):
                rows = pl.ds(r, 8)
                value = combine(lambda i: BL[i, z, rows, :], coefs) + pick(table0, BN[z, rows, :])
                Z[k, z + 1, pl.ds(8 + r, 8), :] = value
                res = R0[z, rows, :]
                for i, coef in enumerate(coefs):
                    res = res - coef * W[i, z, rows, :]
                rz = rz + res * value
                if k > 0:
                    image = W[k - 1, z, rows, :]
                    if k > 1:
                        image = image + other * W[0, z, rows, :]
                    zs = zs + image * value
            return rz, zs

        zero = jnp.zeros((8, NX), f32)
        rz, zs = lax.fori_loop(0, CZ, plane, (zero, zero))
        for side in range(2):
            inside = a > 0 if side == 0 else a < SLABS - 1
            for r in range(0, CY, 8):
                rows = pl.ds(r, 8)
                value = combine(lambda i: HZ[i, side, rows, :], coefs) + pick(table0, HBZ[side, rows, :])
                Z[k, (CZ + 1) * side, pl.ds(8 + r, 8), :] = jnp.where(inside, value, 0.0)
            inside = b > 0 if side == 0 else b < COLS - 1
            value = combine(lambda i: HY[i, side], coefs) + pick(table1 if side == 0 else table0, HBN[side])
            value = jnp.where(inside, value, 0.0)
            for z in range(CZ):
                Z[k, z + 1, pl.ds(7 if side == 0 else 8 + CY, 1), :] = value[z : z + 1, :]
        return total_of(rz), total_of(zs)

    def image(k):
        def plane(z, acc):
            for r in range(0, CY, 8):
                rows, mine = pl.ds(8 + r, 8), pl.ds(r, 8)
                centre = Z[k, z + 1, rows, :]
                value = (
                    CZF[z + 1, mine, :] * Z[k, z + 2, rows, :]
                    + CZF[z, mine, :] * Z[k, z, rows, :]
                    + CYP[z, mine, :] * Z[k, z + 1, pl.ds(9 + r, 8), :]
                    + CYM[z, mine, :] * Z[k, z + 1, pl.ds(7 + r, 8), :]
                    + CXP[z, mine, :] * x_plus(centre)
                    + CXM[z, mine, :] * x_minus(centre)
                )
                value = DG[z, mine, :] * centre - value
                W[k, z, mine, :] = value
                acc = acc + centre * value
            return acc

        return total_of(lax.fori_loop(0, CZ, plane, jnp.zeros((8, NX), f32)))

    def dots_row(values):
        row = jnp.zeros((1, 128), f32)
        for i, value in enumerate(values):
            row = row + jnp.where(lanes_row == 64 + i, value, 0.0)
        return row

    def dot_at(row, i):
        return jnp.sum(jnp.where(lanes_row == 64 + i, row, 0.0), axis=1, keepdims=True)

    for copy in rows_out:
        copy.wait_recv()
    exchange(0, region_sums(R0), jnp.zeros((1, 128), f32))
    lax.fori_loop(0, CY // 8, factor_rows, 0)
    block_solve(R0, BL.at[0])
    halos = send_block_halo(0)

    for copy in bins_out:
        copy.wait_recv()
    low, high = HBZ[0], HBZ[1]
    HBZ[0] = low + jnp.where(low < S_DEV, 84, jnp.where(low < SPAN, 16, jnp.where(low < 36, 32, -32)))
    HBZ[1] = high + jnp.where(high < S_DEV, 88, jnp.where(high < SPAN, 32, jnp.where(high < 36, -16, 32)))
    for z in range(CZ):
        HBN[0, pl.ds(z, 1), :] = HBY[0, z, pl.ds(7, 1), :]
        HBN[1, pl.ds(z, 1), :] = HBY[1, z, pl.ds(0, 1), :] + 92

    tables0, tables1, coefs = [], [], []
    beta1 = gamma = before = power = None
    coefs = []
    for k in range(3):
        t0, t1 = collect(k)
        tables0.append(t0)
        tables1.append(t1)
        if k == 1:
            power, before = dot_at(t1, 0), dot_at(t1, 1)
            alpha0 = before / power
            coefs = [alpha0]
        if k == 2:
            zw, rz, zs = (dot_at(t1, i) for i in range(3))
            beta1 = rz / before
            power, before = zw + 2.0 * beta1 * zs + beta1 * beta1 * power, rz
            alpha1 = before / power
            coefs = [alpha0 + beta1 * alpha1, alpha1]
        for copy in halos:
            copy.wait_recv()
        rz, zs = direction(k, tables0, tables1, coefs, beta1)
        zw = image(k)
        row = dots_row([zw, rz, zs])
        if k < 2:
            exchange(k + 1, region_sums(W.at[k]), row)
            block_solve(W.at[k], BL.at[k + 1])
            halos_next = send_block_halo(k + 1)
            for copy in halos:
                copy.wait_send()
            halos = halos_next
    for copy in halos:
        copy.wait_send()

    M3[...] = row

    def post(n, c):
        ta, tb = partner(n)
        remote(M3, G3.at[me], gs.at[3], gr.at[3], (ta, tb)).start()
        return c

    lax.fori_loop(0, DEVS - 1, post, 0)
    G3[me] = M3[...]
    for copy in halo + bins_out + rows_out:
        copy.wait_send()
    for k in range(3):
        part = M.at[k, pl.ds(0, DEVS - 1)]
        pltpu.make_async_copy(part, part, gs.at[k]).wait()
    part = G3.at[pl.ds(0, DEVS - 1)]
    pltpu.make_async_copy(part, part, gr.at[3]).wait()

    def add(i, acc):
        return acc + G3[pl.ds(8 * i, 8)]

    total = jnp.sum(lax.fori_loop(0, DEVS // 8, add, jnp.zeros((8, 1, 128), f32)), axis=0)
    zw, rz, zs = (dot_at(total, i) for i in range(3))
    beta2 = rz / before
    power = zw + 2.0 * beta2 * zs + beta2 * beta2 * power
    alpha2 = rz / power
    c1 = alpha1 + beta2 * alpha2
    c0 = alpha0 + beta1 * c1

    def finish(z, c):
        for r in range(0, CY, 8):
            rows, inner = pl.ds(r, 8), pl.ds(8 + r, 8)
            out_x[z, rows, :] = c0 * Z[0, z + 1, inner, :] + c1 * Z[1, z + 1, inner, :] + alpha2 * Z[2, z + 1, inner, :]
            out_r[z, rows, :] = R0[z, rows, :] - (
                c0 * W[0, z, rows, :] + c1 * W[1, z, rows, :] + alpha2 * W[2, z, rows, :]
            )
        return c

    lax.fori_loop(0, CZ, finish, 0)
    pltpu.make_async_copy(part, part, gs.at[3]).wait()


def on_device(fraction, source, bubble_label, subdomain, coarse_inverse):
    out = jax.ShapeDtypeStruct(fraction.shape, f32)
    hbm = pl.BlockSpec(memory_space=pl.ANY)
    vmem = pl.BlockSpec(memory_space=pltpu.VMEM)
    block = (CZ, CY, NX)

    def buf(*shape, dtype=f32):
        return pltpu.VMEM(shape, dtype)

    dma = pltpu.SemaphoreType.DMA
    return pl.pallas_call(
        kernel,
        out_shape=(out, out),
        in_specs=[hbm] * 5,
        out_specs=(vmem, vmem),
        scratch_shapes=[
            buf(CZ + 6, 64, NX),
            buf(3, CZ + 4, 64, NX),
            buf(CZ + 2, 64, NX),
            buf(*block),
            buf(*block, dtype=jnp.int32),
            buf(*block, dtype=jnp.int32),
            buf(*block, dtype=jnp.int32),
            buf(SPAN, DEVS * SPAN),
            buf(56, DEVS * SPAN),
            buf(CZ + 1, CY, NX),
            buf(*block),
            buf(*block),
            buf(*block),
            buf(*block),
            buf(*block),
            buf(*block),
            buf(*block),
            buf(3, *block),
            buf(3, *block),
            buf(3, CZ + 2, 48, NX),
            buf(2, CY, NX, dtype=jnp.int32),
            buf(2, CZ, 8, NX, dtype=jnp.int32),
            buf(3, 2, CY, NX),
            buf(3, 2, CZ, NX),
            buf(2, CZ, NX, dtype=jnp.int32),
            buf(3, 2, CZ, NX),
            buf(56, 128),
            buf(48, 256),
            buf(COLS, 48, 128),
            buf(COLS, 48, 128),
            buf(3, DEVS, 2, 128),
            buf(3, DEVS, 2, 128),
            buf(1, 128),
            buf(DEVS, 1, 128),
            dma((5,)),
            dma((8,)),
            dma((8,)),
            dma((4,)),
            dma((4,)),
            dma((2,)),
            dma((2,)),
            dma((3, 4)),
            dma((3, 4)),
            dma((4,)),
            dma((4,)),
        ],
        compiler_params=pltpu.CompilerParams(
            collective_id=0, has_side_effects=True, vmem_limit_bytes=56 * 2**20
        ),
    )(fraction, source, bubble_label, subdomain, coarse_inverse)


def solution(mesh):
    placed = (P("gz", "gy", None),) * 4 + (P(("gz", "gy"), None),)
    return jax.shard_map(
        on_device, mesh=mesh, in_specs=placed, out_specs=(P("gz", "gy", None),) * 2, check_vma=False
    )
```

```python
import functools

import jax
import jax.numpy as jnp
from jax import lax
from jax.experimental import pallas as pl
from jax.experimental.pallas import tpu as pltpu
from jax.sharding import PartitionSpec as P

MESH = pl.DeviceIdType.MESH
CZ, CY, NX = 8, 32, 512
S_DEV, B_DEV = 4, 16
SPAN = S_DEV + B_DEV
SLABS, COLS = 32, 8
DEVS = SLABS * COLS
f32 = jnp.float32


def lanes_of(shape):
    return lax.broadcasted_iota(jnp.int32, shape, len(shape) - 1)


def x_plus(v):
    n = v.shape[-1]
    return jnp.where(lanes_of(v.shape) == n - 1, 0.0, pltpu.roll(v, n - 1, 1))


def x_minus(v):
    return jnp.where(lanes_of(v.shape) == 0, 0.0, pltpu.roll(v, 1, 1))


def kernel(
    frac, src, lab, sub, cinv, out_x, out_r,
    F, NRM, KAP, SRC, LB, SB, BN, CV, CW, CZF, CYP, CYM, CXP, CXM, DG, IV,
    R0, W, BL, Z, HBZ, HBY, HZ, HY, HBN, HYO, T2, X, YB, YS, M, G, M3, G3,
    ld, fs, fr, bsn, brc, cs, cr, ks, kr, gs, gr, met,
):
    a = lax.axis_index("gz")
    b = lax.axis_index("gy")
    me = b * SLABS + a
    here = a * COLS + b
    phys_y, phys_z = a // 8, lax.rem(a, 8)
    up, down = lax.rem(a + 1, SLABS), lax.rem(a + SLABS - 1, SLABS)
    right, left = lax.rem(b + 1, COLS), lax.rem(b + COLS - 1, COLS)

    loads = [
        pltpu.make_async_copy(frac, F.at[pl.ds(3, CZ), pl.ds(16, CY)], ld.at[0]),
        pltpu.make_async_copy(src, SRC, ld.at[1]),
        pltpu.make_async_copy(lab, LB, ld.at[2]),
        pltpu.make_async_copy(sub, SB, ld.at[3]),
        pltpu.make_async_copy(cinv, CV, ld.at[4]),
    ]
    for copy in loads:
        copy.start()

    def partner(k):
        t = lax.rem(me + 1 + k, DEVS)
        return lax.rem(t, SLABS), t // SLABS

    neighbours = [(c, d) for c in (down, a, up) for d in (left, b, right) if c is not a or d is not b]
    across = [(a, lax.rem(b + k, COLS)) for k in range(1, COLS)]
    along_z = [(phys_y * 8 + lax.rem(phys_z + k, 8), b) for k in range(1, 8)]
    along_y = [(lax.rem(phys_y + k, 4) * 8 + phys_z, b) for k in range(1, 4)]
    bar = pltpu.get_barrier_semaphore()
    first_met = neighbours + across + along_z + along_y
    for device in first_met:
        pl.semaphore_signal(bar, inc=1, device_id=device, device_id_type=MESH)
    pl.semaphore_wait(bar, len(first_met))

    def join(i, group):
        for device in group:
            pl.semaphore_signal(met.at[i], inc=1, device_id=device, device_id_type=MESH)

    def remote(source, target, send, recv, device):
        return pltpu.make_async_remote_copy(
            src_ref=source, dst_ref=target, send_sem=send, recv_sem=recv, device_id=device, device_id_type=MESH
        )

    halo = [
        remote(frac.at[pl.ds(0, 3)], F.at[pl.ds(11, 3), pl.ds(16, CY)], fs.at[0], fr.at[0], (down, b)),
        remote(frac.at[pl.ds(5, 3)], F.at[pl.ds(0, 3), pl.ds(16, CY)], fs.at[1], fr.at[1], (up, b)),
        remote(frac.at[:, pl.ds(24, 8)], F.at[pl.ds(3, CZ), pl.ds(8, 8)], fs.at[2], fr.at[2], (a, right)),
        remote(frac.at[:, pl.ds(0, 8)], F.at[pl.ds(3, CZ), pl.ds(48, 8)], fs.at[3], fr.at[3], (a, left)),
        remote(frac.at[pl.ds(6, 2), pl.ds(24, 8)], F.at[pl.ds(1, 2), pl.ds(8, 8)], fs.at[4], fr.at[4], (up, right)),
        remote(frac.at[pl.ds(6, 2), pl.ds(0, 8)], F.at[pl.ds(1, 2), pl.ds(48, 8)], fs.at[5], fr.at[5], (up, left)),
        remote(frac.at[pl.ds(0, 2), pl.ds(24, 8)], F.at[pl.ds(11, 2), pl.ds(8, 8)], fs.at[6], fr.at[6], (down, right)),
        remote(frac.at[pl.ds(0, 2), pl.ds(0, 8)], F.at[pl.ds(11, 2), pl.ds(48, 8)], fs.at[7], fr.at[7], (down, left)),
    ]
    for copy in halo:
        copy.start()
    join(0, across)

    loads[2].wait()
    loads[3].wait()

    def bins_plane(z, c):
        label, domain = LB[z], SB[z]
        off = (label >> 7) - a
        shift = jnp.where(off == 0, S_DEV, jnp.where(off < 0, SPAN, SPAN + B_DEV))
        BN[z] = jnp.where(label >= 0, (label & 15) + shift, domain - here * S_DEV)
        return c

    lax.fori_loop(0, CZ, bins_plane, 0)
    bins_out = [
        remote(BN.at[0], HBZ.at[1], bsn.at[0], brc.at[0], (down, b)),
        remote(BN.at[CZ - 1], HBZ.at[0], bsn.at[1], brc.at[1], (up, b)),
        remote(BN.at[:, pl.ds(24, 8)], HBY.at[0], bsn.at[2], brc.at[2], (a, right)),
        remote(BN.at[:, pl.ds(0, 8)], HBY.at[1], bsn.at[3], brc.at[3], (a, left)),
    ]
    for copy in bins_out:
        copy.start()

    loads[4].wait()
    first = CV[pl.ds(0, 8), :]
    CW[pl.ds(0, 8), :] = jnp.where(lax.broadcasted_iota(jnp.int32, first.shape, 0) < S_DEV, first, 0.0)
    CW[pl.ds(8, B_DEV), :] = CV[pl.ds(S_DEV, B_DEV), :]
    rows_out = [
        remote(CW.at[pl.ds(8, B_DEV)], CW.at[pl.ds(24, B_DEV)], cs.at[0], cr.at[0], (up, b)),
        remote(CW.at[pl.ds(8, B_DEV)], CW.at[pl.ds(40, B_DEV)], cs.at[1], cr.at[1], (down, b)),
    ]
    for copy in rows_out:
        copy.start()
    pl.semaphore_wait(met.at[0], len(across))
    join(1, along_z)
    X[...] = jnp.zeros_like(X)
    YB[...] = jnp.zeros_like(YB)
    YS[...] = jnp.zeros_like(YS)
    T2[...] = jnp.zeros_like(T2)

    loads[0].wait()
    loads[1].wait()
    for copy in halo:
        copy.wait_recv()
    pl.semaphore_wait(met.at[1], len(along_z))
    join(2, along_y)

    @pl.when(a == 0)
    def _():
        F[pl.ds(0, 3)] = jnp.zeros((3,) + F.shape[1:], f32)

    @pl.when(a == SLABS - 1)
    def _():
        F[pl.ds(11, 3)] = jnp.zeros((3,) + F.shape[1:], f32)

    @pl.when(b == 0)
    def _():
        F[:, pl.ds(8, 8)] = jnp.zeros((F.shape[0], 8, NX), f32)

    @pl.when(b == COLS - 1)
    def _():
        F[:, pl.ds(48, 8)] = jnp.zeros((F.shape[0], 8, NX), f32)

    def row_valid(first_row, shape):
        row = lax.broadcasted_iota(jnp.int32, shape, 0) + (first_row - 16 + b * CY)
        return (row >= 0) & (row < COLS * CY)

    def z_valid(z):
        place = a * CZ + z
        return (place >= 0) & (place < SLABS * CZ)

    wide = (8, 24, 40)

    def normals_plane(n, c):
        inside = z_valid(n - 2)
        for r in wide:
            rows = pl.ds(r, 16)
            centre = F[n + 1, rows, :]
            gz = 0.5 * (F[n + 2, rows, :] - F[n, rows, :])
            gy = 0.5 * (F[n + 1, pl.ds(r + 1, 16), :] - F[n + 1, pl.ds(r - 1, 16), :])
            gx = 0.5 * (x_plus(centre) - x_minus(centre))
            scale = jnp.minimum(lax.rsqrt(gz * gz + gy * gy + gx * gx), 4.0)
            scale = jnp.where(row_valid(r, scale.shape) & inside, scale, 0.0)
            NRM[0, n, rows, :] = gz * scale
            NRM[1, n, rows, :] = gy * scale
            NRM[2, n, rows, :] = gx * scale
        return c

    lax.fori_loop(0, CZ + 4, normals_plane, 0)

    def kappa_plane(n, c):
        inside = z_valid(n - 1)
        for r in wide:
            rows = pl.ds(r, 16)
            nx = NRM[2, n + 1, rows, :]
            value = -(
                0.5 * (NRM[0, n + 2, rows, :] - NRM[0, n, rows, :])
                + 0.5 * (NRM[1, n + 1, pl.ds(r + 1, 16), :] - NRM[1, n + 1, pl.ds(r - 1, 16), :])
                + 0.5 * (x_plus(nx) - x_minus(nx))
            )
            KAP[n, rows, :] = jnp.where(row_valid(r, value.shape) & inside, value, 0.0)
        return c

    lax.fori_loop(0, CZ + 2, kappa_plane, 0)

    def density(v):
        return 1.0 - 0.75 * v

    def faces_plane(n, c):
        for r in (0, 16):
            rows = pl.ds(16 + r, 16)
            CZF[n, pl.ds(r, 16), :] = 2.0 / (density(F[n + 2, rows, :]) + density(F[n + 3, rows, :]))
        return c

    lax.fori_loop(0, CZ + 1, faces_plane, 0)

    def assemble_plane(z, c):
        for r in range(0, CY, 8):
            rows, mine = pl.ds(16 + r, 8), pl.ds(r, 8)
            fc, kc = F[z + 3, rows, :], KAP[z + 1, rows, :]
            dc = density(fc)
            fy = (F[z + 3, pl.ds(17 + r, 8), :], F[z + 3, pl.ds(15 + r, 8), :])
            fx = (x_plus(fc), x_minus(fc))
            cz = (CZF[z + 1, mine, :], CZF[z, mine, :])
            cy = tuple(2.0 / (dc + density(v)) for v in fy)
            cx = tuple(2.0 / (dc + density(v)) for v in fx)
            CYP[z, mine, :], CYM[z, mine, :] = cy
            CXP[z, mine, :], CXM[z, mine, :] = cx
            DG[z, mine, :] = 0.05 + (cz[0] + cz[1] + cy[0] + cy[1] + cx[0] + cx[1])
            term = cz[0] * (0.5 * (kc + KAP[z + 2, rows, :])) * (F[z + 4, rows, :] - fc)
            term = term + cz[1] * (0.5 * (kc + KAP[z, rows, :])) * (F[z + 2, rows, :] - fc)
            term = term + cy[0] * (0.5 * (kc + KAP[z + 1, pl.ds(17 + r, 8), :])) * (fy[0] - fc)
            term = term + cy[1] * (0.5 * (kc + KAP[z + 1, pl.ds(15 + r, 8), :])) * (fy[1] - fc)
            term = term + cx[0] * (0.5 * (kc + x_plus(kc))) * (fx[0] - fc)
            term = term + cx[1] * (0.5 * (kc + x_minus(kc))) * (fx[1] - fc)
            R0[z, mine, :] = SRC[z, mine, :] - 0.5 * term
        return c

    lax.fori_loop(0, CZ, assemble_plane, 0)

    def factor_rows(i, c):
        rows = pl.ds(pl.multiple_of(i * 8, 8), 8)
        inverse = 1.0 / DG[0, rows, :]
        IV[0, rows, :] = inverse
        for z in range(1, CZ):
            face = CZF[z, rows, :]
            inverse = 1.0 / (DG[z, rows, :] - (face * inverse) * face)
            IV[z, rows, :] = inverse
        return c

    lanes_row = lanes_of((1, 128))

    def region_sums(v_ref):
        for group in range(3):
            base = S_DEV + B_DEV * group

            def tile(t, acc, base=base, group=group):
                z, rows = t // 4, pl.ds(pl.multiple_of(lax.rem(t, 4) * 8, 8), 8)
                bins, v = BN[z, rows, :], v_ref[z, rows, :]
                new = []
                for k in range(B_DEV):
                    picked = jnp.where(bins == base + k, v, 0.0)
                    new.append(
                        acc[k]
                        + ((picked[:, 0:128] + picked[:, 128:256]) + (picked[:, 256:384] + picked[:, 384:512]))
                    )
                return tuple(new)

            acc = lax.fori_loop(0, CZ * 4, tile, tuple(jnp.zeros((8, 128), f32) for _ in range(B_DEV)))
            for k in range(B_DEV):
                T2[pl.ds(8 + B_DEV * group + k, 1), :] = jnp.sum(acc[k], axis=0, keepdims=True)

        def liquid(t, acc):
            z, rows = t // 4, pl.ds(pl.multiple_of(lax.rem(t, 4) * 8, 8), 8)
            return acc + jnp.where(BN[z, rows, :] < S_DEV, v_ref[z, rows, :], 0.0)

        acc = lax.fori_loop(0, CZ * 4, liquid, jnp.zeros((8, NX), f32))
        domain = SB[0, pl.ds(0, 8), :] - here * S_DEV
        for k in range(S_DEV):
            picked = jnp.sum(jnp.where(domain == k, acc, 0.0), axis=0, keepdims=True)
            T2[pl.ds(k, 1), :] = (picked[:, 0:128] + picked[:, 128:256]) + (picked[:, 256:384] + picked[:, 384:512])
        return jnp.sum(T2[...], axis=1, keepdims=True)

    def exchange(k, sums, dots):
        for g in range(8):
            part = jnp.sum(CW[:, pl.ds(640 * g, 640)] * sums, axis=0, keepdims=True)
            for j in range(4):
                moved = part if j == 0 else pltpu.roll(part, 640 - 160 * j, 1)
                X[pl.ds(8 + 4 * g + j, 1), :] = moved[:, 0:256]
        wide_lanes = lanes_of((SLABS, 128))
        rows = pl.ds(8, SLABS)
        for t in range(COLS):
            if t <= 5:
                moved = X[rows, pl.ds(0, 128)]
                moved = moved if t == 0 else pltpu.roll(moved, 128 - SPAN * t, 1)
            elif t == 6:
                moved = pltpu.roll(X[rows, :], 256 - SPAN * t, 1)[:, 0:128]
            else:
                moved = pltpu.roll(X[rows, pl.ds(128, 128)], 256 - SPAN * t, 1)
            YS[t, rows, :] = jnp.where(wide_lanes < S_DEV, moved, 0.0)
            YB[t, rows, :] = jnp.where((wide_lanes >= S_DEV) & (wide_lanes < SPAN), moved, 0.0)
        before = None
        for t in range(COLS):
            row0 = (
                (YS[t, rows, :] + YB[t, rows, :])
                + pltpu.roll(YB[t, pl.ds(7, SLABS), :], 16, 1)
                + pltpu.roll(YB[t, pl.ds(9, SLABS), :], 32, 1)
                + pltpu.roll(YB[t, pl.ds(6, SLABS), :], 48, 1)
                + pltpu.roll(YB[t, pl.ds(10, SLABS), :], 64, 1)
                + pltpu.roll(YS[t, pl.ds(7, SLABS), :], 84, 1)
                + pltpu.roll(YS[t, pl.ds(9, SLABS), :], 88, 1)
            )
            if t + 1 < COLS:
                row0 = row0 + pltpu.roll(YS[t + 1, rows, :], 92, 1)
            row1 = jnp.broadcast_to(dots, (SLABS, 128))
            if before is not None:
                row1 = row1 + jnp.where(wide_lanes < SPAN + 2 * B_DEV, before, 0.0)
            M[k, pl.ds(SLABS * t, SLABS), 0, :] = row0
            M[k, pl.ds(SLABS * t, SLABS), 1, :] = row1
            before = row0

        def post(n, c):
            ta, tb = partner(n)
            remote(M.at[k, tb * SLABS + ta], G.at[k, me], gs.at[k], gr.at[k], (ta, tb)).start()
            return c

        lax.fori_loop(0, DEVS - 1, post, 0)
        G[k, me] = M[k, me]

    def collect(k):
        part = G.at[k, pl.ds(0, DEVS - 1)]
        pltpu.make_async_copy(part, part, gr.at[k]).wait()

        def add(i, acc):
            return acc + G[k, pl.ds(8 * i, 8)]

        total = jnp.sum(lax.fori_loop(0, DEVS // 8, add, jnp.zeros((8, 2, 128), f32)), axis=0)
        return total[0:1, :], total[1:2, :]

    def block_solve(v_ref, o_ref):
        def solve_rows(i, c):
            rows = pl.ds(pl.multiple_of(i * 8, 8), 8)
            inv = [IV[z, rows, :] for z in range(CZ)]
            face = [CZF[z, rows, :] for z in range(1, CZ)]
            held = [v_ref[0, rows, :] * inv[0]]
            for z in range(1, CZ):
                held.append((v_ref[z, rows, :] + face[z - 1] * held[z - 1]) * inv[z])
            value = held[CZ - 1]
            o_ref[CZ - 1, rows, :] = value
            for z in range(CZ - 2, -1, -1):
                value = held[z] + (face[z] * value) * inv[z]
                o_ref[z, rows, :] = value
            return c

        lax.fori_loop(0, CY // 8, solve_rows, 0)

    def send_block_halo(k):
        o_ref = BL.at[k]
        for z in range(CZ):
            HYO[k, 0, pl.ds(z, 1), :] = BL[k, z, pl.ds(CY - 1, 1), :]
            HYO[k, 1, pl.ds(z, 1), :] = BL[k, z, pl.ds(0, 1), :]
        out = [
            remote(o_ref.at[0], HZ.at[k, 1], ks.at[k, 0], kr.at[k, 0], (down, b)),
            remote(o_ref.at[CZ - 1], HZ.at[k, 0], ks.at[k, 1], kr.at[k, 1], (up, b)),
            remote(HYO.at[k, 0], HY.at[k, 0], ks.at[k, 2], kr.at[k, 2], (a, right)),
            remote(HYO.at[k, 1], HY.at[k, 1], ks.at[k, 3], kr.at[k, 3], (a, left)),
        ]
        for copy in out:
            copy.start()
        return out

    def pick(table, bins):
        rows = bins.shape[0]
        spread = jnp.broadcast_to(table, (rows, 128))
        return jnp.concatenate(
            [
                jnp.take_along_axis(spread, bins[:, 128 * i : 128 * i + 128], axis=1, mode="promise_in_bounds")
                for i in range(NX // 128)
            ],
            axis=1,
        )

    def combine(ref_at, coefs):
        value = ref_at(0)
        for i, coef in enumerate(coefs):
            value = value - coef * ref_at(i + 1)
        return value

    def total_of(acc):
        part = jnp.sum(acc, axis=0, keepdims=True)
        return jnp.sum(part, axis=1, keepdims=True)

    def direction(k, tables0, tables1, coefs, other):
        table0 = combine(lambda i: tables0[i], coefs)
        table1 = combine(lambda i: tables1[i], coefs)

        def plane(z, acc):
            rz, zs = acc
            for r in range(0, CY, 8):
                rows = pl.ds(r, 8)
                value = combine(lambda i: BL[i, z, rows, :], coefs) + pick(table0, BN[z, rows, :])
                Z[k, z + 1, pl.ds(8 + r, 8), :] = value
                res = R0[z, rows, :]
                for i, coef in enumerate(coefs):
                    res = res - coef * W[i, z, rows, :]
                rz = rz + res * value
                if k > 0:
                    image = W[k - 1, z, rows, :]
                    if k > 1:
                        image = image + other * W[0, z, rows, :]
                    zs = zs + image * value
            return rz, zs

        zero = jnp.zeros((8, NX), f32)
        rz, zs = lax.fori_loop(0, CZ, plane, (zero, zero))
        for side in range(2):
            inside = a > 0 if side == 0 else a < SLABS - 1
            for r in range(0, CY, 8):
                rows = pl.ds(r, 8)
                value = combine(lambda i: HZ[i, side, rows, :], coefs) + pick(table0, HBZ[side, rows, :])
                Z[k, (CZ + 1) * side, pl.ds(8 + r, 8), :] = jnp.where(inside, value, 0.0)
            inside = b > 0 if side == 0 else b < COLS - 1
            value = combine(lambda i: HY[i, side], coefs) + pick(table1 if side == 0 else table0, HBN[side])
            value = jnp.where(inside, value, 0.0)
            for z in range(CZ):
                Z[k, z + 1, pl.ds(7 if side == 0 else 8 + CY, 1), :] = value[z : z + 1, :]
        return total_of(rz), total_of(zs)

    def image(k):
        def plane(z, acc):
            for r in range(0, CY, 8):
                rows, mine = pl.ds(8 + r, 8), pl.ds(r, 8)
                centre = Z[k, z + 1, rows, :]
                value = (
                    CZF[z + 1, mine, :] * Z[k, z + 2, rows, :]
                    + CZF[z, mine, :] * Z[k, z, rows, :]
                    + CYP[z, mine, :] * Z[k, z + 1, pl.ds(9 + r, 8), :]
                    + CYM[z, mine, :] * Z[k, z + 1, pl.ds(7 + r, 8), :]
                    + CXP[z, mine, :] * x_plus(centre)
                    + CXM[z, mine, :] * x_minus(centre)
                )
                value = DG[z, mine, :] * centre - value
                W[k, z, mine, :] = value
                acc = acc + centre * value
            return acc

        return total_of(lax.fori_loop(0, CZ, plane, jnp.zeros((8, NX), f32)))

    def dots_row(values):
        row = jnp.zeros((1, 128), f32)
        for i, value in enumerate(values):
            row = row + jnp.where(lanes_row == 64 + i, value, 0.0)
        return row

    def dot_at(row, i):
        return jnp.sum(jnp.where(lanes_row == 64 + i, row, 0.0), axis=1, keepdims=True)

    sums = region_sums(R0)
    for copy in rows_out:
        copy.wait_recv()
    pl.semaphore_wait(met.at[2], len(along_y))
    exchange(0, sums, jnp.zeros((1, 128), f32))
    lax.fori_loop(0, CY // 8, factor_rows, 0)
    block_solve(R0, BL.at[0])
    halos = send_block_halo(0)

    for copy in bins_out:
        copy.wait_recv()
    low, high = HBZ[0], HBZ[1]
    HBZ[0] = low + jnp.where(low < S_DEV, 84, jnp.where(low < SPAN, 16, jnp.where(low < 36, 32, -32)))
    HBZ[1] = high + jnp.where(high < S_DEV, 88, jnp.where(high < SPAN, 32, jnp.where(high < 36, -16, 32)))
    for z in range(CZ):
        HBN[0, pl.ds(z, 1), :] = HBY[0, z, pl.ds(7, 1), :]
        HBN[1, pl.ds(z, 1), :] = HBY[1, z, pl.ds(0, 1), :] + 92

    tables0, tables1, coefs = [], [], []
    beta1 = gamma = before = power = None
    coefs = []
    for k in range(3):
        t0, t1 = collect(k)
        tables0.append(t0)
        tables1.append(t1)
        if k == 1:
            power, before = dot_at(t1, 0), dot_at(t1, 1)
            alpha0 = before / power
            coefs = [alpha0]
        if k == 2:
            zw, rz, zs = (dot_at(t1, i) for i in range(3))
            beta1 = rz / before
            power, before = zw + 2.0 * beta1 * zs + beta1 * beta1 * power, rz
            alpha1 = before / power
            coefs = [alpha0 + beta1 * alpha1, alpha1]
        for copy in halos:
            copy.wait_recv()
        rz, zs = direction(k, tables0, tables1, coefs, beta1)
        zw = image(k)
        row = dots_row([zw, rz, zs])
        if k < 2:
            exchange(k + 1, region_sums(W.at[k]), row)
            block_solve(W.at[k], BL.at[k + 1])
            halos_next = send_block_halo(k + 1)
            for copy in halos:
                copy.wait_send()
            halos = halos_next
    for copy in halos:
        copy.wait_send()

    M3[...] = row

    def post(n, c):
        ta, tb = partner(n)
        remote(M3, G3.at[me], gs.at[3], gr.at[3], (ta, tb)).start()
        return c

    lax.fori_loop(0, DEVS - 1, post, 0)
    G3[me] = M3[...]
    for copy in halo + bins_out + rows_out:
        copy.wait_send()
    for k in range(3):
        part = M.at[k, pl.ds(0, DEVS - 1)]
        pltpu.make_async_copy(part, part, gs.at[k]).wait()
    part = G3.at[pl.ds(0, DEVS - 1)]
    pltpu.make_async_copy(part, part, gr.at[3]).wait()

    def add(i, acc):
        return acc + G3[pl.ds(8 * i, 8)]

    total = jnp.sum(lax.fori_loop(0, DEVS // 8, add, jnp.zeros((8, 1, 128), f32)), axis=0)
    zw, rz, zs = (dot_at(total, i) for i in range(3))
    beta2 = rz / before
    power = zw + 2.0 * beta2 * zs + beta2 * beta2 * power
    alpha2 = rz / power
    c1 = alpha1 + beta2 * alpha2
    c0 = alpha0 + beta1 * c1

    def finish(z, c):
        for r in range(0, CY, 8):
            rows, inner = pl.ds(r, 8), pl.ds(8 + r, 8)
            out_x[z, rows, :] = c0 * Z[0, z + 1, inner, :] + c1 * Z[1, z + 1, inner, :] + alpha2 * Z[2, z + 1, inner, :]
            out_r[z, rows, :] = R0[z, rows, :] - (
                c0 * W[0, z, rows, :] + c1 * W[1, z, rows, :] + alpha2 * W[2, z, rows, :]
            )
        return c

    lax.fori_loop(0, CZ, finish, 0)
    pltpu.make_async_copy(part, part, gs.at[3]).wait()


def on_device(fraction, source, bubble_label, subdomain, coarse_inverse):
    out = jax.ShapeDtypeStruct(fraction.shape, f32)
    hbm = pl.BlockSpec(memory_space=pl.ANY)
    vmem = pl.BlockSpec(memory_space=pltpu.VMEM)
    block = (CZ, CY, NX)

    def buf(*shape, dtype=f32):
        return pltpu.VMEM(shape, dtype)

    dma = pltpu.SemaphoreType.DMA
    return pl.pallas_call(
        kernel,
        out_shape=(out, out),
        in_specs=[hbm] * 5,
        out_specs=(vmem, vmem),
        scratch_shapes=[
            buf(CZ + 6, 64, NX),
            buf(3, CZ + 4, 64, NX),
            buf(CZ + 2, 64, NX),
            buf(*block),
            buf(*block, dtype=jnp.int32),
            buf(*block, dtype=jnp.int32),
            buf(*block, dtype=jnp.int32),
            buf(SPAN, DEVS * SPAN),
            buf(56, DEVS * SPAN),
            buf(CZ + 1, CY, NX),
            buf(*block),
            buf(*block),
            buf(*block),
            buf(*block),
            buf(*block),
            buf(*block),
            buf(*block),
            buf(3, *block),
            buf(3, *block),
            buf(3, CZ + 2, 48, NX),
            buf(2, CY, NX, dtype=jnp.int32),
            buf(2, CZ, 8, NX, dtype=jnp.int32),
            buf(3, 2, CY, NX),
            buf(3, 2, CZ, NX),
            buf(2, CZ, NX, dtype=jnp.int32),
            buf(3, 2, CZ, NX),
            buf(56, 128),
            buf(48, 256),
            buf(COLS, 48, 128),
            buf(COLS, 48, 128),
            buf(3, DEVS, 2, 128),
            buf(3, DEVS, 2, 128),
            buf(1, 128),
            buf(DEVS, 1, 128),
            dma((5,)),
            dma((8,)),
            dma((8,)),
            dma((4,)),
            dma((4,)),
            dma((2,)),
            dma((2,)),
            dma((3, 4)),
            dma((3, 4)),
            dma((4,)),
            dma((4,)),
            pltpu.SemaphoreType.REGULAR((3,)),
        ],
        compiler_params=pltpu.CompilerParams(
            collective_id=0, has_side_effects=True, vmem_limit_bytes=56 * 2**20
        ),
    )(fraction, source, bubble_label, subdomain, coarse_inverse)


def solution(mesh):
    placed = (P("gz", "gy", None),) * 4 + (P(("gz", "gy"), None),)
    return jax.shard_map(
        on_device, mesh=mesh, in_specs=placed, out_specs=(P("gz", "gy", None),) * 2, check_vma=False
    )
```

```python
import functools

import jax
import jax.numpy as jnp
from jax import lax
from jax.experimental import pallas as pl
from jax.experimental.pallas import tpu as pltpu
from jax.sharding import PartitionSpec as P

MESH = pl.DeviceIdType.MESH
CZ, CY, NX = 8, 32, 512
S_DEV, B_DEV = 4, 16
SPAN = S_DEV + B_DEV
SLABS, COLS = 32, 8
DEVS = SLABS * COLS
f32 = jnp.float32


def lanes_of(shape):
    return lax.broadcasted_iota(jnp.int32, shape, len(shape) - 1)


def x_plus(v):
    n = v.shape[-1]
    return jnp.where(lanes_of(v.shape) == n - 1, 0.0, pltpu.roll(v, n - 1, 1))


def x_minus(v):
    return jnp.where(lanes_of(v.shape) == 0, 0.0, pltpu.roll(v, 1, 1))


def kernel(
    frac, src, lab, sub, cinv, out_x, out_r,
    F, PK, PG, NRM, KAP, SRC, LB, SB, BN, CV, CW, CZF, CYP, CYM, CXP, CXM, DG, IV,
    R0, W, BL, Z, HBZ, HBY, HZ, HY, HBN, HYO, T2, X, YB, YS, M, G, M3, G3,
    ld, fs, fr, bsn, brc, cs, cr, ks, kr, gs, gr, met,
):
    a = lax.axis_index("gz")
    b = lax.axis_index("gy")
    me = b * SLABS + a
    here = a * COLS + b
    phys_y, phys_z = a // 8, lax.rem(a, 8)
    up, down = lax.rem(a + 1, SLABS), lax.rem(a + SLABS - 1, SLABS)
    right, left = lax.rem(b + 1, COLS), lax.rem(b + COLS - 1, COLS)

    loads = [
        pltpu.make_async_copy(frac, F.at[pl.ds(3, CZ), pl.ds(16, CY)], ld.at[0]),
        pltpu.make_async_copy(src, SRC, ld.at[1]),
        pltpu.make_async_copy(lab, LB, ld.at[2]),
        pltpu.make_async_copy(sub, SB, ld.at[3]),
        pltpu.make_async_copy(cinv, CV, ld.at[4]),
    ]
    for copy in loads:
        copy.start()

    def everyone(post):
        for away in (4, 3, 5, 2, 6, 1, 7, 0):
            there = lax.rem(phys_z + away, 8)

            def one(n, c, there=there):
                t = lax.rem(phys_y * COLS + b + 1 + n, 4 * COLS)
                post(((t // COLS) * 8 + there, lax.rem(t, COLS)))
                return c

            lax.fori_loop(0, 4 * COLS - (away == 0), one, 0)

    neighbours = [(c, d) for c in (down, a, up) for d in (left, b, right) if c is not a or d is not b]
    across = [(a, lax.rem(b + k, COLS)) for k in range(1, COLS)]
    along_z = [(phys_y * 8 + lax.rem(phys_z + k, 8), b) for k in range(1, 8)]
    along_y = [(lax.rem(phys_y + k, 4) * 8 + phys_z, b) for k in range(1, 4)]
    corners = (
        (((10, 47), (10, 46), (9, 47)), ((2, 15), (2, 14), (1, 15))),
        (((10, 16), (10, 17), (9, 16)), ((2, 48), (2, 49), (1, 48))),
        (((3, 47), (3, 46), (4, 47)), ((11, 15), (11, 14), (12, 15))),
        (((3, 16), (3, 17), (4, 16)), ((11, 48), (11, 49), (12, 48))),
    )
    bar = pltpu.get_barrier_semaphore()
    first_met = neighbours + across + along_z + along_y
    for device in first_met:
        pl.semaphore_signal(bar, inc=1, device_id=device, device_id_type=MESH)
    loads[0].wait()
    PK[...] = jnp.zeros_like(PK)
    for i, (mine, _) in enumerate(corners):
        for j, (z, y) in enumerate(mine):
            PK[i, pl.ds(j, 1), :] = F[z, pl.ds(y, 1), :]
    pl.semaphore_wait(bar, len(first_met))

    def join(i, group):
        for device in group:
            pl.semaphore_signal(met.at[i], inc=1, device_id=device, device_id_type=MESH)

    def remote(source, target, send, recv, device):
        return pltpu.make_async_remote_copy(
            src_ref=source, dst_ref=target, send_sem=send, recv_sem=recv, device_id=device, device_id_type=MESH
        )

    halo = [
        remote(frac.at[pl.ds(0, 3)], F.at[pl.ds(11, 3), pl.ds(16, CY)], fs.at[0], fr.at[0], (down, b)),
        remote(frac.at[pl.ds(5, 3)], F.at[pl.ds(0, 3), pl.ds(16, CY)], fs.at[1], fr.at[1], (up, b)),
        remote(frac.at[:, pl.ds(24, 8)], F.at[pl.ds(3, CZ), pl.ds(8, 8)], fs.at[2], fr.at[2], (a, right)),
        remote(frac.at[:, pl.ds(0, 8)], F.at[pl.ds(3, CZ), pl.ds(48, 8)], fs.at[3], fr.at[3], (a, left)),
        remote(PK.at[0], PG.at[0], fs.at[4], fr.at[4], (up, right)),
        remote(PK.at[1], PG.at[1], fs.at[5], fr.at[5], (up, left)),
        remote(PK.at[2], PG.at[2], fs.at[6], fr.at[6], (down, right)),
        remote(PK.at[3], PG.at[3], fs.at[7], fr.at[7], (down, left)),
    ]
    for copy in halo:
        copy.start()
    join(0, across)

    loads[2].wait()
    loads[3].wait()

    def bins_plane(z, c):
        label, domain = LB[z], SB[z]
        off = (label >> 7) - a
        shift = jnp.where(off == 0, S_DEV, jnp.where(off < 0, SPAN, SPAN + B_DEV))
        BN[z] = jnp.where(label >= 0, (label & 15) + shift, domain - here * S_DEV)
        return c

    lax.fori_loop(0, CZ, bins_plane, 0)
    bins_out = [
        remote(BN.at[0], HBZ.at[1], bsn.at[0], brc.at[0], (down, b)),
        remote(BN.at[CZ - 1], HBZ.at[0], bsn.at[1], brc.at[1], (up, b)),
        remote(BN.at[:, pl.ds(24, 8)], HBY.at[0], bsn.at[2], brc.at[2], (a, right)),
        remote(BN.at[:, pl.ds(0, 8)], HBY.at[1], bsn.at[3], brc.at[3], (a, left)),
    ]
    for copy in bins_out:
        copy.start()

    loads[4].wait()
    first = CV[pl.ds(0, 8), :]
    CW[pl.ds(0, 8), :] = jnp.where(lax.broadcasted_iota(jnp.int32, first.shape, 0) < S_DEV, first, 0.0)
    CW[pl.ds(8, B_DEV), :] = CV[pl.ds(S_DEV, B_DEV), :]
    rows_out = [
        remote(CW.at[pl.ds(8, B_DEV)], CW.at[pl.ds(24, B_DEV)], cs.at[0], cr.at[0], (up, b)),
        remote(CW.at[pl.ds(8, B_DEV)], CW.at[pl.ds(40, B_DEV)], cs.at[1], cr.at[1], (down, b)),
    ]
    for copy in rows_out:
        copy.start()
    pl.semaphore_wait(met.at[0], len(across))
    join(1, along_z)
    X[...] = jnp.zeros_like(X)
    YB[...] = jnp.zeros_like(YB)
    YS[...] = jnp.zeros_like(YS)
    T2[...] = jnp.zeros_like(T2)

    def row_valid(first_row, shape):
        row = lax.broadcasted_iota(jnp.int32, shape, 0) + (first_row - 16 + b * CY)
        return (row >= 0) & (row < COLS * CY)

    def z_valid(z):
        place = a * CZ + z
        return (place >= 0) & (place < SLABS * CZ)

    wide = (8, 24, 40)

    def normals_plane(n, c):
        inside = z_valid(n - 2)
        for r in wide:
            rows = pl.ds(r, 16)
            centre = F[n + 1, rows, :]
            gz = 0.5 * (F[n + 2, rows, :] - F[n, rows, :])
            gy = 0.5 * (F[n + 1, pl.ds(r + 1, 16), :] - F[n + 1, pl.ds(r - 1, 16), :])
            gx = 0.5 * (x_plus(centre) - x_minus(centre))
            scale = jnp.minimum(lax.rsqrt(gz * gz + gy * gy + gx * gx), 4.0)
            scale = jnp.where(row_valid(r, scale.shape) & inside, scale, 0.0)
            NRM[0, n, rows, :] = gz * scale
            NRM[1, n, rows, :] = gy * scale
            NRM[2, n, rows, :] = gx * scale
        return c

    def kappa_plane(n, c):
        inside = z_valid(n - 1)
        for r in wide:
            rows = pl.ds(r, 16)
            nx = NRM[2, n + 1, rows, :]
            value = -(
                0.5 * (NRM[0, n + 2, rows, :] - NRM[0, n, rows, :])
                + 0.5 * (NRM[1, n + 1, pl.ds(r + 1, 16), :] - NRM[1, n + 1, pl.ds(r - 1, 16), :])
                + 0.5 * (x_plus(nx) - x_minus(nx))
            )
            KAP[n, rows, :] = jnp.where(row_valid(r, value.shape) & inside, value, 0.0)
        return c

    def density(v):
        return 1.0 - 0.75 * v

    def faces_plane(n, c):
        for r in (0, 16):
            rows = pl.ds(16 + r, 16)
            CZF[n, pl.ds(r, 16), :] = 2.0 / (density(F[n + 2, rows, :]) + density(F[n + 3, rows, :]))
        return c

    def assemble_plane(z, c):
        for r in range(0, CY, 8):
            rows, mine = pl.ds(16 + r, 8), pl.ds(r, 8)
            fc, kc = F[z + 3, rows, :], KAP[z + 1, rows, :]
            dc = density(fc)
            fy = (F[z + 3, pl.ds(17 + r, 8), :], F[z + 3, pl.ds(15 + r, 8), :])
            fx = (x_plus(fc), x_minus(fc))
            cz = (CZF[z + 1, mine, :], CZF[z, mine, :])
            cy = tuple(2.0 / (dc + density(v)) for v in fy)
            cx = tuple(2.0 / (dc + density(v)) for v in fx)
            CYP[z, mine, :], CYM[z, mine, :] = cy
            CXP[z, mine, :], CXM[z, mine, :] = cx
            DG[z, mine, :] = 0.05 + (cz[0] + cz[1] + cy[0] + cy[1] + cx[0] + cx[1])
            term = cz[0] * (0.5 * (kc + KAP[z + 2, rows, :])) * (F[z + 4, rows, :] - fc)
            term = term + cz[1] * (0.5 * (kc + KAP[z, rows, :])) * (F[z + 2, rows, :] - fc)
            term = term + cy[0] * (0.5 * (kc + KAP[z + 1, pl.ds(17 + r, 8), :])) * (fy[0] - fc)
            term = term + cy[1] * (0.5 * (kc + KAP[z + 1, pl.ds(15 + r, 8), :])) * (fy[1] - fc)
            term = term + cx[0] * (0.5 * (kc + x_plus(kc))) * (fx[0] - fc)
            term = term + cx[1] * (0.5 * (kc + x_minus(kc))) * (fx[1] - fc)
            R0[z, mine, :] = SRC[z, mine, :] - 0.5 * term
        return c

    loads[1].wait()
    halo[2].wait_recv()
    halo[3].wait_recv()

    def clear_rows(first, count):
        @pl.when(b == 0)
        def _():
            F[pl.ds(first, count), pl.ds(8, 8)] = jnp.zeros((count, 8, NX), f32)

        @pl.when(b == COLS - 1)
        def _():
            F[pl.ds(first, count), pl.ds(48, 8)] = jnp.zeros((count, 8, NX), f32)

    clear_rows(3, CZ)
    lax.fori_loop(3, 9, normals_plane, 0)
    lax.fori_loop(3, 7, kappa_plane, 0)
    lax.fori_loop(1, CZ, faces_plane, 0)
    lax.fori_loop(3, 5, assemble_plane, 0)

    for i in (0, 1, 4, 5, 6, 7):
        halo[i].wait_recv()
    for i, (_, theirs) in enumerate(corners):
        for j, (z, y) in enumerate(theirs):
            F[z, pl.ds(y, 1), :] = PG[i, pl.ds(j, 1), :]
    pl.semaphore_wait(met.at[1], len(along_z))
    join(2, along_y)
    clear_rows(0, 3)
    clear_rows(11, 3)

    @pl.when(a == 0)
    def _():
        F[pl.ds(0, 3)] = jnp.zeros((3,) + F.shape[1:], f32)

    @pl.when(a == SLABS - 1)
    def _():
        F[pl.ds(11, 3)] = jnp.zeros((3,) + F.shape[1:], f32)

    def outer(n, count, step):
        return n + step * (n // count)

    lax.fori_loop(0, 6, lambda n, c: normals_plane(outer(n, 3, 6), c), 0)
    lax.fori_loop(0, 6, lambda n, c: kappa_plane(outer(n, 3, 4), c), 0)
    lax.fori_loop(0, 2, lambda n, c: faces_plane(n * CZ, c), 0)
    lax.fori_loop(0, 6, lambda n, c: assemble_plane(outer(n, 3, 2), c), 0)

    def factor_rows(i, c):
        rows = pl.ds(pl.multiple_of(i * 8, 8), 8)
        inverse = 1.0 / DG[0, rows, :]
        IV[0, rows, :] = inverse
        for z in range(1, CZ):
            face = CZF[z, rows, :]
            inverse = 1.0 / (DG[z, rows, :] - (face * inverse) * face)
            IV[z, rows, :] = inverse
        return c

    lanes_row = lanes_of((1, 128))

    def region_sums(v_ref):
        for group in range(3):
            base = S_DEV + B_DEV * group

            def tile(t, acc, base=base, group=group):
                z, rows = t // 4, pl.ds(pl.multiple_of(lax.rem(t, 4) * 8, 8), 8)
                bins, v = BN[z, rows, :], v_ref[z, rows, :]
                new = []
                for k in range(B_DEV):
                    picked = jnp.where(bins == base + k, v, 0.0)
                    new.append(
                        acc[k]
                        + ((picked[:, 0:128] + picked[:, 128:256]) + (picked[:, 256:384] + picked[:, 384:512]))
                    )
                return tuple(new)

            acc = lax.fori_loop(0, CZ * 4, tile, tuple(jnp.zeros((8, 128), f32) for _ in range(B_DEV)), unroll=4)
            for k in range(B_DEV):
                T2[pl.ds(8 + B_DEV * group + k, 1), :] = jnp.sum(acc[k], axis=0, keepdims=True)

        def liquid(t, acc):
            z, rows = t // 4, pl.ds(pl.multiple_of(lax.rem(t, 4) * 8, 8), 8)
            return acc + jnp.where(BN[z, rows, :] < S_DEV, v_ref[z, rows, :], 0.0)

        acc = lax.fori_loop(0, CZ * 4, liquid, jnp.zeros((8, NX), f32))
        domain = SB[0, pl.ds(0, 8), :] - here * S_DEV
        for k in range(S_DEV):
            picked = jnp.sum(jnp.where(domain == k, acc, 0.0), axis=0, keepdims=True)
            T2[pl.ds(k, 1), :] = (picked[:, 0:128] + picked[:, 128:256]) + (picked[:, 256:384] + picked[:, 384:512])

    def exchange(k, count, dots):
        sums = jnp.sum(T2[pl.ds(0, count), :], axis=1, keepdims=True)
        for g in range(8):
            part = jnp.sum(CW[pl.ds(0, count), pl.ds(640 * g, 640)] * sums, axis=0, keepdims=True)
            for j in range(4):
                moved = part if j == 0 else pltpu.roll(part, 640 - 160 * j, 1)
                X[pl.ds(8 + 4 * g + j, 1), :] = moved[:, 0:256]
        wide_lanes = lanes_of((SLABS, 128))
        rows = pl.ds(8, SLABS)
        for t in range(COLS):
            if t <= 5:
                moved = X[rows, pl.ds(0, 128)]
                moved = moved if t == 0 else pltpu.roll(moved, 128 - SPAN * t, 1)
            elif t == 6:
                moved = pltpu.roll(X[rows, :], 256 - SPAN * t, 1)[:, 0:128]
            else:
                moved = pltpu.roll(X[rows, pl.ds(128, 128)], 256 - SPAN * t, 1)
            YS[t, rows, :] = jnp.where(wide_lanes < S_DEV, moved, 0.0)
            YB[t, rows, :] = jnp.where((wide_lanes >= S_DEV) & (wide_lanes < SPAN), moved, 0.0)
        before = None
        for t in range(COLS):
            row0 = (
                (YS[t, rows, :] + YB[t, rows, :])
                + pltpu.roll(YB[t, pl.ds(7, SLABS), :], 16, 1)
                + pltpu.roll(YB[t, pl.ds(9, SLABS), :], 32, 1)
                + pltpu.roll(YB[t, pl.ds(6, SLABS), :], 48, 1)
                + pltpu.roll(YB[t, pl.ds(10, SLABS), :], 64, 1)
                + pltpu.roll(YS[t, pl.ds(7, SLABS), :], 84, 1)
                + pltpu.roll(YS[t, pl.ds(9, SLABS), :], 88, 1)
            )
            if t + 1 < COLS:
                row0 = row0 + pltpu.roll(YS[t + 1, rows, :], 92, 1)
            row1 = jnp.broadcast_to(dots, (SLABS, 128))
            if before is not None:
                row1 = row1 + jnp.where(wide_lanes < SPAN + 2 * B_DEV, before, 0.0)
            M[k, pl.ds(SLABS * t, SLABS), 0, :] = row0
            M[k, pl.ds(SLABS * t, SLABS), 1, :] = row1
            before = row0

        def post(device):
            remote(M.at[k, device[1] * SLABS + device[0]], G.at[k, me], gs.at[k], gr.at[k], device).start()

        everyone(post)
        G[k, me] = M[k, me]

    def collect(k):
        part = G.at[k, pl.ds(0, DEVS - 1)]
        pltpu.make_async_copy(part, part, gr.at[k]).wait()

        def add(i, acc):
            return acc + G[k, pl.ds(8 * i, 8)]

        total = jnp.sum(lax.fori_loop(0, DEVS // 8, add, jnp.zeros((8, 2, 128), f32)), axis=0)
        return total[0:1, :], total[1:2, :]

    def block_solve(v_ref, o_ref):
        def solve_rows(i, c):
            rows = pl.ds(pl.multiple_of(i * 8, 8), 8)
            inv = [IV[z, rows, :] for z in range(CZ)]
            face = [CZF[z, rows, :] for z in range(1, CZ)]
            held = [v_ref[0, rows, :] * inv[0]]
            for z in range(1, CZ):
                held.append((v_ref[z, rows, :] + face[z - 1] * held[z - 1]) * inv[z])
            value = held[CZ - 1]
            o_ref[CZ - 1, rows, :] = value
            for z in range(CZ - 2, -1, -1):
                value = held[z] + (face[z] * value) * inv[z]
                o_ref[z, rows, :] = value
            return c

        lax.fori_loop(0, CY // 8, solve_rows, 0)

    def send_block_halo(k):
        o_ref = BL.at[k]
        for z in range(CZ):
            HYO[k, 0, pl.ds(z, 1), :] = BL[k, z, pl.ds(CY - 1, 1), :]
            HYO[k, 1, pl.ds(z, 1), :] = BL[k, z, pl.ds(0, 1), :]
        out = [
            remote(o_ref.at[0], HZ.at[k, 1], ks.at[k, 0], kr.at[k, 0], (down, b)),
            remote(o_ref.at[CZ - 1], HZ.at[k, 0], ks.at[k, 1], kr.at[k, 1], (up, b)),
            remote(HYO.at[k, 0], HY.at[k, 0], ks.at[k, 2], kr.at[k, 2], (a, right)),
            remote(HYO.at[k, 1], HY.at[k, 1], ks.at[k, 3], kr.at[k, 3], (a, left)),
        ]
        for copy in out:
            copy.start()
        return out

    def pick(table, bins):
        rows = bins.shape[0]
        spread = jnp.broadcast_to(table, (rows, 128))
        return jnp.concatenate(
            [
                jnp.take_along_axis(spread, bins[:, 128 * i : 128 * i + 128], axis=1, mode="promise_in_bounds")
                for i in range(NX // 128)
            ],
            axis=1,
        )

    def combine(ref_at, coefs):
        value = ref_at(0)
        for i, coef in enumerate(coefs):
            value = value - coef * ref_at(i + 1)
        return value

    def total_of(acc):
        part = jnp.sum(acc, axis=0, keepdims=True)
        return jnp.sum(part, axis=1, keepdims=True)

    def direction(k, tables0, tables1, coefs, other):
        table0 = combine(lambda i: tables0[i], coefs)
        table1 = combine(lambda i: tables1[i], coefs)

        def plane(z, acc):
            rz, zs = acc
            for r in range(0, CY, 8):
                rows = pl.ds(r, 8)
                value = combine(lambda i: BL[i, z, rows, :], coefs) + pick(table0, BN[z, rows, :])
                Z[k, z + 1, pl.ds(8 + r, 8), :] = value
                res = R0[z, rows, :]
                for i, coef in enumerate(coefs):
                    res = res - coef * W[i, z, rows, :]
                rz = rz + res * value
                if k > 0:
                    image = W[k - 1, z, rows, :]
                    if k > 1:
                        image = image + other * W[0, z, rows, :]
                    zs = zs + image * value
            return rz, zs

        zero = jnp.zeros((8, NX), f32)
        rz, zs = lax.fori_loop(0, CZ, plane, (zero, zero))
        for side in range(2):
            inside = a > 0 if side == 0 else a < SLABS - 1
            for r in range(0, CY, 8):
                rows = pl.ds(r, 8)
                value = combine(lambda i: HZ[i, side, rows, :], coefs) + pick(table0, HBZ[side, rows, :])
                Z[k, (CZ + 1) * side, pl.ds(8 + r, 8), :] = jnp.where(inside, value, 0.0)
            inside = b > 0 if side == 0 else b < COLS - 1
            value = combine(lambda i: HY[i, side], coefs) + pick(table1 if side == 0 else table0, HBN[side])
            value = jnp.where(inside, value, 0.0)
            for z in range(CZ):
                Z[k, z + 1, pl.ds(7 if side == 0 else 8 + CY, 1), :] = value[z : z + 1, :]
        return total_of(rz), total_of(zs)

    def image(k):
        def plane(z, acc):
            for r in range(0, CY, 8):
                rows, mine = pl.ds(8 + r, 8), pl.ds(r, 8)
                centre = Z[k, z + 1, rows, :]
                value = (
                    CZF[z + 1, mine, :] * Z[k, z + 2, rows, :]
                    + CZF[z, mine, :] * Z[k, z, rows, :]
                    + CYP[z, mine, :] * Z[k, z + 1, pl.ds(9 + r, 8), :]
                    + CYM[z, mine, :] * Z[k, z + 1, pl.ds(7 + r, 8), :]
                    + CXP[z, mine, :] * x_plus(centre)
                    + CXM[z, mine, :] * x_minus(centre)
                )
                value = DG[z, mine, :] * centre - value
                W[k, z, mine, :] = value
                acc = acc + centre * value
            return acc

        return total_of(lax.fori_loop(0, CZ, plane, jnp.zeros((8, NX), f32)))

    def dots_row(values):
        row = jnp.zeros((1, 128), f32)
        for i, value in enumerate(values):
            row = row + jnp.where(lanes_row == 64 + i, value, 0.0)
        return row

    def dot_at(row, i):
        return jnp.sum(jnp.where(lanes_row == 64 + i, row, 0.0), axis=1, keepdims=True)

    region_sums(R0)
    pl.semaphore_wait(met.at[2], len(along_y))
    for copy in rows_out:
        copy.wait_recv()
    exchange(0, 56, jnp.zeros((1, 128), f32))
    lax.fori_loop(0, CY // 8, factor_rows, 0)
    block_solve(R0, BL.at[0])
    halos = send_block_halo(0)

    for copy in bins_out:
        copy.wait_recv()
    low, high = HBZ[0], HBZ[1]
    HBZ[0] = low + jnp.where(low < S_DEV, 84, jnp.where(low < SPAN, 16, jnp.where(low < 36, 32, -32)))
    HBZ[1] = high + jnp.where(high < S_DEV, 88, jnp.where(high < SPAN, 32, jnp.where(high < 36, -16, 32)))
    for z in range(CZ):
        HBN[0, pl.ds(z, 1), :] = HBY[0, z, pl.ds(7, 1), :]
        HBN[1, pl.ds(z, 1), :] = HBY[1, z, pl.ds(0, 1), :] + 92

    tables0, tables1, coefs = [], [], []
    beta1 = gamma = before = power = None
    coefs = []
    for k in range(3):
        t0, t1 = collect(k)
        tables0.append(t0)
        tables1.append(t1)
        if k == 1:
            power, before = dot_at(t1, 0), dot_at(t1, 1)
            alpha0 = before / power
            coefs = [alpha0]
        if k == 2:
            zw, rz, zs = (dot_at(t1, i) for i in range(3))
            beta1 = rz / before
            power, before = zw + 2.0 * beta1 * zs + beta1 * beta1 * power, rz
            alpha1 = before / power
            coefs = [alpha0 + beta1 * alpha1, alpha1]
        for copy in halos:
            copy.wait_recv()
        rz, zs = direction(k, tables0, tables1, coefs, beta1)
        zw = image(k)
        row = dots_row([zw, rz, zs])
        if k < 2:
            region_sums(W.at[k])
            exchange(k + 1, 56, row)
            block_solve(W.at[k], BL.at[k + 1])
            halos_next = send_block_halo(k + 1)
            for copy in halos:
                copy.wait_send()
            halos = halos_next
    for copy in halos:
        copy.wait_send()

    M3[...] = row

    everyone(lambda device: remote(M3, G3.at[me], gs.at[3], gr.at[3], device).start())
    G3[me] = M3[...]
    for copy in halo + bins_out + rows_out:
        copy.wait_send()
    for k in range(3):
        part = M.at[k, pl.ds(0, DEVS - 1)]
        pltpu.make_async_copy(part, part, gs.at[k]).wait()
    part = G3.at[pl.ds(0, DEVS - 1)]
    pltpu.make_async_copy(part, part, gr.at[3]).wait()

    def add(i, acc):
        return acc + G3[pl.ds(8 * i, 8)]

    total = jnp.sum(lax.fori_loop(0, DEVS // 8, add, jnp.zeros((8, 1, 128), f32)), axis=0)
    zw, rz, zs = (dot_at(total, i) for i in range(3))
    beta2 = rz / before
    power = zw + 2.0 * beta2 * zs + beta2 * beta2 * power
    alpha2 = rz / power
    c1 = alpha1 + beta2 * alpha2
    c0 = alpha0 + beta1 * c1

    def finish(z, c):
        for r in range(0, CY, 8):
            rows, inner = pl.ds(r, 8), pl.ds(8 + r, 8)
            out_x[z, rows, :] = c0 * Z[0, z + 1, inner, :] + c1 * Z[1, z + 1, inner, :] + alpha2 * Z[2, z + 1, inner, :]
            out_r[z, rows, :] = R0[z, rows, :] - (
                c0 * W[0, z, rows, :] + c1 * W[1, z, rows, :] + alpha2 * W[2, z, rows, :]
            )
        return c

    lax.fori_loop(0, CZ, finish, 0)
    pltpu.make_async_copy(part, part, gs.at[3]).wait()


def on_device(fraction, source, bubble_label, subdomain, coarse_inverse):
    out = jax.ShapeDtypeStruct(fraction.shape, f32)
    hbm = pl.BlockSpec(memory_space=pl.ANY)
    vmem = pl.BlockSpec(memory_space=pltpu.VMEM)
    block = (CZ, CY, NX)

    def buf(*shape, dtype=f32):
        return pltpu.VMEM(shape, dtype)

    dma = pltpu.SemaphoreType.DMA
    return pl.pallas_call(
        kernel,
        out_shape=(out, out),
        in_specs=[hbm] * 5,
        out_specs=(vmem, vmem),
        scratch_shapes=[
            buf(CZ + 6, 64, NX),
            buf(4, 4, NX),
            buf(4, 4, NX),
            buf(3, CZ + 4, 64, NX),
            buf(CZ + 2, 64, NX),
            buf(*block),
            buf(*block, dtype=jnp.int32),
            buf(*block, dtype=jnp.int32),
            buf(*block, dtype=jnp.int32),
            buf(SPAN, DEVS * SPAN),
            buf(56, DEVS * SPAN),
            buf(CZ + 1, CY, NX),
            buf(*block),
            buf(*block),
            buf(*block),
            buf(*block),
            buf(*block),
            buf(*block),
            buf(*block),
            buf(3, *block),
            buf(3, *block),
            buf(3, CZ + 2, 48, NX),
            buf(2, CY, NX, dtype=jnp.int32),
            buf(2, CZ, 8, NX, dtype=jnp.int32),
            buf(3, 2, CY, NX),
            buf(3, 2, CZ, NX),
            buf(2, CZ, NX, dtype=jnp.int32),
            buf(3, 2, CZ, NX),
            buf(56, 128),
            buf(48, 256),
            buf(COLS, 48, 128),
            buf(COLS, 48, 128),
            buf(3, DEVS, 2, 128),
            buf(3, DEVS, 2, 128),
            buf(1, 128),
            buf(DEVS, 1, 128),
            dma((5,)),
            dma((8,)),
            dma((8,)),
            dma((4,)),
            dma((4,)),
            dma((2,)),
            dma((2,)),
            dma((3, 4)),
            dma((3, 4)),
            dma((4,)),
            dma((4,)),
            pltpu.SemaphoreType.REGULAR((3,)),
        ],
        compiler_params=pltpu.CompilerParams(
            collective_id=0, has_side_effects=True, vmem_limit_bytes=56 * 2**20
        ),
    )(fraction, source, bubble_label, subdomain, coarse_inverse)


def solution(mesh):
    placed = (P("gz", "gy", None),) * 4 + (P(("gz", "gy"), None),)
    return jax.shard_map(
        on_device, mesh=mesh, in_specs=placed, out_specs=(P("gz", "gy", None),) * 2, check_vma=False
    )
```

```python
import functools

import jax
import jax.numpy as jnp
from jax import lax
from jax.experimental import pallas as pl
from jax.experimental.pallas import tpu as pltpu
from jax.sharding import PartitionSpec as P

MESH = pl.DeviceIdType.MESH
CZ, CY, NX = 8, 32, 512
S_DEV, B_DEV = 4, 16
SPAN = S_DEV + B_DEV
SLABS, COLS = 32, 8
DEVS = SLABS * COLS
f32 = jnp.float32


def lanes_of(shape):
    return lax.broadcasted_iota(jnp.int32, shape, len(shape) - 1)


def x_plus(v):
    n = v.shape[-1]
    return jnp.where(lanes_of(v.shape) == n - 1, 0.0, pltpu.roll(v, n - 1, 1))


def x_minus(v):
    return jnp.where(lanes_of(v.shape) == 0, 0.0, pltpu.roll(v, 1, 1))


def kernel(
    frac, src, lab, sub, cinv, out_x, out_r,
    F, PK, PG, NRM, KAP, SRC, LB, SB, BN, CV, CW, CZF, CYP, CYM, CXP, CXM, DG, IV,
    R0, W, BL, Z, HBZ, HBY, HZ, HY, HBN, HYO, T2, X, YB, YS, M, G, M3, G3,
    ld, fs, fr, bsn, brc, cs, cr, ks, kr, gs, gr, met,
):
    a = lax.axis_index("gz")
    b = lax.axis_index("gy")
    me = b * SLABS + a
    here = a * COLS + b
    phys_y, phys_z = a // 8, lax.rem(a, 8)
    up, down = lax.rem(a + 1, SLABS), lax.rem(a + SLABS - 1, SLABS)
    right, left = lax.rem(b + 1, COLS), lax.rem(b + COLS - 1, COLS)

    loads = [
        pltpu.make_async_copy(frac, F.at[pl.ds(3, CZ), pl.ds(16, CY)], ld.at[0]),
        pltpu.make_async_copy(src, SRC, ld.at[1]),
        pltpu.make_async_copy(lab, LB, ld.at[2]),
        pltpu.make_async_copy(sub, SB, ld.at[3]),
        pltpu.make_async_copy(cinv, CV, ld.at[4]),
    ]
    for copy in loads:
        copy.start()

    def everyone(post):
        for away in (4, 3, 5, 2, 6, 1, 7, 0):
            there = lax.rem(phys_z + away, 8)

            def one(n, c, there=there):
                t = lax.rem(phys_y * COLS + b + 1 + n, 4 * COLS)
                post((lax.div(t, COLS) * 8 + there, lax.rem(t, COLS)))
                return c

            lax.fori_loop(0, 4 * COLS - (away == 0), one, 0)

    neighbours = [(c, d) for c in (down, a, up) for d in (left, b, right) if c is not a or d is not b]
    across = [(a, lax.rem(b + k, COLS)) for k in range(1, COLS)]
    along_z = [(phys_y * 8 + lax.rem(phys_z + k, 8), b) for k in range(1, 8)]
    along_y = [(lax.rem(phys_y + k, 4) * 8 + phys_z, b) for k in range(1, 4)]
    corners = (
        (((10, 47), (10, 46), (9, 47)), ((2, 15), (2, 14), (1, 15))),
        (((10, 16), (10, 17), (9, 16)), ((2, 48), (2, 49), (1, 48))),
        (((3, 47), (3, 46), (4, 47)), ((11, 15), (11, 14), (12, 15))),
        (((3, 16), (3, 17), (4, 16)), ((11, 48), (11, 49), (12, 48))),
    )
    bar = pltpu.get_barrier_semaphore()
    first_met = neighbours + across + along_z + along_y
    for device in first_met:
        pl.semaphore_signal(bar, inc=1, device_id=device, device_id_type=MESH)
    loads[0].wait()
    PK[...] = jnp.zeros_like(PK)
    for i, (mine, _) in enumerate(corners):
        for j, (z, y) in enumerate(mine):
            PK[i, pl.ds(j, 1), :] = F[z, pl.ds(y, 1), :]
    loads[2].wait()
    loads[3].wait()

    def bins_plane(z, c):
        label, domain = LB[z], SB[z]
        off = (label >> 7) - a
        shift = jnp.where(off == 0, S_DEV, jnp.where(off < 0, SPAN, SPAN + B_DEV))
        BN[z] = jnp.where(label >= 0, (label & 15) + shift, domain - here * S_DEV)
        return c

    lax.fori_loop(0, CZ, bins_plane, 0)
    loads[4].wait()
    first = CV[pl.ds(0, 8), :]
    CW[pl.ds(0, 8), :] = jnp.where(lax.broadcasted_iota(jnp.int32, first.shape, 0) < S_DEV, first, 0.0)
    CW[pl.ds(8, B_DEV), :] = CV[pl.ds(S_DEV, B_DEV), :]
    X[...] = jnp.zeros_like(X)
    YB[...] = jnp.zeros_like(YB)
    YS[...] = jnp.zeros_like(YS)
    T2[...] = jnp.zeros_like(T2)

    pl.semaphore_wait(bar, len(first_met))

    def join(i, group):
        for device in group:
            pl.semaphore_signal(met.at[i], inc=1, device_id=device, device_id_type=MESH)

    def remote(source, target, send, recv, device):
        return pltpu.make_async_remote_copy(
            src_ref=source, dst_ref=target, send_sem=send, recv_sem=recv, device_id=device, device_id_type=MESH
        )

    halo = [
        remote(frac.at[pl.ds(0, 3)], F.at[pl.ds(11, 3), pl.ds(16, CY)], fs.at[0], fr.at[0], (down, b)),
        remote(frac.at[pl.ds(5, 3)], F.at[pl.ds(0, 3), pl.ds(16, CY)], fs.at[1], fr.at[1], (up, b)),
        remote(frac.at[:, pl.ds(24, 8)], F.at[pl.ds(3, CZ), pl.ds(8, 8)], fs.at[2], fr.at[2], (a, right)),
        remote(frac.at[:, pl.ds(0, 8)], F.at[pl.ds(3, CZ), pl.ds(48, 8)], fs.at[3], fr.at[3], (a, left)),
        remote(PK.at[0], PG.at[0], fs.at[4], fr.at[4], (up, right)),
        remote(PK.at[1], PG.at[1], fs.at[5], fr.at[5], (up, left)),
        remote(PK.at[2], PG.at[2], fs.at[6], fr.at[6], (down, right)),
        remote(PK.at[3], PG.at[3], fs.at[7], fr.at[7], (down, left)),
    ]
    for copy in halo:
        copy.start()
    join(0, across)

    bins_out = [
        remote(BN.at[0], HBZ.at[1], bsn.at[0], brc.at[0], (down, b)),
        remote(BN.at[CZ - 1], HBZ.at[0], bsn.at[1], brc.at[1], (up, b)),
        remote(BN.at[:, pl.ds(24, 8)], HBY.at[0], bsn.at[2], brc.at[2], (a, right)),
        remote(BN.at[:, pl.ds(0, 8)], HBY.at[1], bsn.at[3], brc.at[3], (a, left)),
    ]
    for copy in bins_out:
        copy.start()

    rows_out = [
        remote(CW.at[pl.ds(8, B_DEV)], CW.at[pl.ds(24, B_DEV)], cs.at[0], cr.at[0], (up, b)),
        remote(CW.at[pl.ds(8, B_DEV)], CW.at[pl.ds(40, B_DEV)], cs.at[1], cr.at[1], (down, b)),
    ]
    for copy in rows_out:
        copy.start()
    pl.semaphore_wait(met.at[0], len(across))
    join(1, along_z)
    def row_valid(first_row, shape):
        row = lax.broadcasted_iota(jnp.int32, shape, 0) + (first_row - 16 + b * CY)
        return (row >= 0) & (row < COLS * CY)

    def z_valid(z):
        place = a * CZ + z
        return (place >= 0) & (place < SLABS * CZ)

    wide = (8, 24, 40)

    def normals_plane(n, c):
        inside = z_valid(n - 2)
        for r in wide:
            rows = pl.ds(r, 16)
            centre = F[n + 1, rows, :]
            gz = 0.5 * (F[n + 2, rows, :] - F[n, rows, :])
            gy = 0.5 * (F[n + 1, pl.ds(r + 1, 16), :] - F[n + 1, pl.ds(r - 1, 16), :])
            gx = 0.5 * (x_plus(centre) - x_minus(centre))
            scale = jnp.minimum(lax.rsqrt(gz * gz + gy * gy + gx * gx), 4.0)
            scale = jnp.where(row_valid(r, scale.shape) & inside, scale, 0.0)
            NRM[0, n, rows, :] = gz * scale
            NRM[1, n, rows, :] = gy * scale
            NRM[2, n, rows, :] = gx * scale
        return c

    def kappa_plane(n, c):
        inside = z_valid(n - 1)
        for r in wide:
            rows = pl.ds(r, 16)
            nx = NRM[2, n + 1, rows, :]
            value = -(
                0.5 * (NRM[0, n + 2, rows, :] - NRM[0, n, rows, :])
                + 0.5 * (NRM[1, n + 1, pl.ds(r + 1, 16), :] - NRM[1, n + 1, pl.ds(r - 1, 16), :])
                + 0.5 * (x_plus(nx) - x_minus(nx))
            )
            KAP[n, rows, :] = jnp.where(row_valid(r, value.shape) & inside, value, 0.0)
        return c

    def density(v):
        return 1.0 - 0.75 * v

    def faces_plane(n, c):
        for r in (0, 16):
            rows = pl.ds(16 + r, 16)
            CZF[n, pl.ds(r, 16), :] = 2.0 / (density(F[n + 2, rows, :]) + density(F[n + 3, rows, :]))
        return c

    def assemble_plane(z, c):
        for r in range(0, CY, 8):
            rows, mine = pl.ds(16 + r, 8), pl.ds(r, 8)
            fc, kc = F[z + 3, rows, :], KAP[z + 1, rows, :]
            dc = density(fc)
            fy = (F[z + 3, pl.ds(17 + r, 8), :], F[z + 3, pl.ds(15 + r, 8), :])
            fx = (x_plus(fc), x_minus(fc))
            cz = (CZF[z + 1, mine, :], CZF[z, mine, :])
            cy = tuple(2.0 / (dc + density(v)) for v in fy)
            cx = tuple(2.0 / (dc + density(v)) for v in fx)
            CYP[z, mine, :], CYM[z, mine, :] = cy
            CXP[z, mine, :], CXM[z, mine, :] = cx
            DG[z, mine, :] = 0.05 + (cz[0] + cz[1] + cy[0] + cy[1] + cx[0] + cx[1])
            term = cz[0] * (0.5 * (kc + KAP[z + 2, rows, :])) * (F[z + 4, rows, :] - fc)
            term = term + cz[1] * (0.5 * (kc + KAP[z, rows, :])) * (F[z + 2, rows, :] - fc)
            term = term + cy[0] * (0.5 * (kc + KAP[z + 1, pl.ds(17 + r, 8), :])) * (fy[0] - fc)
            term = term + cy[1] * (0.5 * (kc + KAP[z + 1, pl.ds(15 + r, 8), :])) * (fy[1] - fc)
            term = term + cx[0] * (0.5 * (kc + x_plus(kc))) * (fx[0] - fc)
            term = term + cx[1] * (0.5 * (kc + x_minus(kc))) * (fx[1] - fc)
            R0[z, mine, :] = SRC[z, mine, :] - 0.5 * term
        return c

    loads[1].wait()
    halo[2].wait_recv()
    halo[3].wait_recv()

    def clear_rows(first, count):
        @pl.when(b == 0)
        def _():
            F[pl.ds(first, count), pl.ds(8, 8)] = jnp.zeros((count, 8, NX), f32)

        @pl.when(b == COLS - 1)
        def _():
            F[pl.ds(first, count), pl.ds(48, 8)] = jnp.zeros((count, 8, NX), f32)

    clear_rows(3, CZ)
    lax.fori_loop(3, 9, normals_plane, 0)
    lax.fori_loop(3, 7, kappa_plane, 0)
    lax.fori_loop(1, CZ, faces_plane, 0)
    lax.fori_loop(3, 5, assemble_plane, 0)

    for i in (0, 1, 4, 5, 6, 7):
        halo[i].wait_recv()
    for i, (_, theirs) in enumerate(corners):
        for j, (z, y) in enumerate(theirs):
            F[z, pl.ds(y, 1), :] = PG[i, pl.ds(j, 1), :]
    pl.semaphore_wait(met.at[1], len(along_z))
    join(2, along_y)
    clear_rows(0, 3)
    clear_rows(11, 3)

    @pl.when(a == 0)
    def _():
        F[pl.ds(0, 3)] = jnp.zeros((3,) + F.shape[1:], f32)

    @pl.when(a == SLABS - 1)
    def _():
        F[pl.ds(11, 3)] = jnp.zeros((3,) + F.shape[1:], f32)

    def outer(n, count, step):
        return n + step * (n // count)

    lax.fori_loop(0, 6, lambda n, c: normals_plane(outer(n, 3, 6), c), 0)
    lax.fori_loop(0, 6, lambda n, c: kappa_plane(outer(n, 3, 4), c), 0)
    lax.fori_loop(0, 2, lambda n, c: faces_plane(n * CZ, c), 0)
    lax.fori_loop(0, 6, lambda n, c: assemble_plane(outer(n, 3, 2), c), 0)

    def factor_rows(i, c):
        rows = pl.ds(pl.multiple_of(i * 8, 8), 8)
        inverse = 1.0 / DG[0, rows, :]
        IV[0, rows, :] = inverse
        for z in range(1, CZ):
            face = CZF[z, rows, :]
            inverse = 1.0 / (DG[z, rows, :] - (face * inverse) * face)
            IV[z, rows, :] = inverse
        return c

    lanes_row = lanes_of((1, 128))

    def region_sums(v_ref):
        for group in range(3):
            base = S_DEV + B_DEV * group

            def tile(t, acc, base=base, group=group):
                z, rows = t // 4, pl.ds(pl.multiple_of(lax.rem(t, 4) * 8, 8), 8)
                bins, v = BN[z, rows, :], v_ref[z, rows, :]
                new = []
                for k in range(B_DEV):
                    picked = jnp.where(bins == base + k, v, 0.0)
                    new.append(
                        acc[k]
                        + ((picked[:, 0:128] + picked[:, 128:256]) + (picked[:, 256:384] + picked[:, 384:512]))
                    )
                return tuple(new)

            acc = lax.fori_loop(0, CZ * 4, tile, tuple(jnp.zeros((8, 128), f32) for _ in range(B_DEV)), unroll=8)
            for k in range(B_DEV):
                T2[pl.ds(8 + B_DEV * group + k, 1), :] = jnp.sum(acc[k], axis=0, keepdims=True)

        def liquid(t, acc):
            z, rows = t // 4, pl.ds(pl.multiple_of(lax.rem(t, 4) * 8, 8), 8)
            return acc + jnp.where(BN[z, rows, :] < S_DEV, v_ref[z, rows, :], 0.0)

        acc = lax.fori_loop(0, CZ * 4, liquid, jnp.zeros((8, NX), f32))
        domain = SB[0, pl.ds(0, 8), :] - here * S_DEV
        for k in range(S_DEV):
            picked = jnp.sum(jnp.where(domain == k, acc, 0.0), axis=0, keepdims=True)
            T2[pl.ds(k, 1), :] = (picked[:, 0:128] + picked[:, 128:256]) + (picked[:, 256:384] + picked[:, 384:512])

    def exchange(k, count, dots):
        sums = jnp.sum(T2[pl.ds(0, count), :], axis=1, keepdims=True)
        for g in range(8):
            part = jnp.sum(CW[pl.ds(0, count), pl.ds(640 * g, 640)] * sums, axis=0, keepdims=True)
            for j in range(4):
                moved = part if j == 0 else pltpu.roll(part, 640 - 160 * j, 1)
                X[pl.ds(8 + 4 * g + j, 1), :] = moved[:, 0:256]
        wide_lanes = lanes_of((SLABS, 128))
        rows = pl.ds(8, SLABS)
        for t in range(COLS):
            if t <= 5:
                moved = X[rows, pl.ds(0, 128)]
                moved = moved if t == 0 else pltpu.roll(moved, 128 - SPAN * t, 1)
            elif t == 6:
                moved = pltpu.roll(X[rows, :], 256 - SPAN * t, 1)[:, 0:128]
            else:
                moved = pltpu.roll(X[rows, pl.ds(128, 128)], 256 - SPAN * t, 1)
            YS[t, rows, :] = jnp.where(wide_lanes < S_DEV, moved, 0.0)
            YB[t, rows, :] = jnp.where((wide_lanes >= S_DEV) & (wide_lanes < SPAN), moved, 0.0)
        before = None
        for t in range(COLS):
            row0 = (
                (YS[t, rows, :] + YB[t, rows, :])
                + pltpu.roll(YB[t, pl.ds(7, SLABS), :], 16, 1)
                + pltpu.roll(YB[t, pl.ds(9, SLABS), :], 32, 1)
                + pltpu.roll(YB[t, pl.ds(6, SLABS), :], 48, 1)
                + pltpu.roll(YB[t, pl.ds(10, SLABS), :], 64, 1)
                + pltpu.roll(YS[t, pl.ds(7, SLABS), :], 84, 1)
                + pltpu.roll(YS[t, pl.ds(9, SLABS), :], 88, 1)
            )
            if t + 1 < COLS:
                row0 = row0 + pltpu.roll(YS[t + 1, rows, :], 92, 1)
            row1 = jnp.broadcast_to(dots, (SLABS, 128))
            if before is not None:
                row1 = row1 + jnp.where(wide_lanes < SPAN + 2 * B_DEV, before, 0.0)
            M[k, pl.ds(SLABS * t, SLABS), 0, :] = row0
            M[k, pl.ds(SLABS * t, SLABS), 1, :] = row1
            before = row0

        def post(device):
            remote(M.at[k, device[1] * SLABS + device[0]], G.at[k, me], gs.at[k], gr.at[k], device).start()

        everyone(post)
        G[k, me] = M[k, me]

    def collect(k):
        part = G.at[k, pl.ds(0, DEVS - 1)]
        pltpu.make_async_copy(part, part, gr.at[k]).wait()

        def add(i, acc):
            return acc + G[k, pl.ds(8 * i, 8)]

        total = jnp.sum(lax.fori_loop(0, DEVS // 8, add, jnp.zeros((8, 2, 128), f32)), axis=0)
        return total[0:1, :], total[1:2, :]

    def block_solve(v_ref, o_ref):
        def solve_rows(i, c):
            rows = pl.ds(pl.multiple_of(i * 8, 8), 8)
            inv = [IV[z, rows, :] for z in range(CZ)]
            face = [CZF[z, rows, :] for z in range(1, CZ)]
            held = [v_ref[0, rows, :] * inv[0]]
            for z in range(1, CZ):
                held.append((v_ref[z, rows, :] + face[z - 1] * held[z - 1]) * inv[z])
            value = held[CZ - 1]
            o_ref[CZ - 1, rows, :] = value
            for z in range(CZ - 2, -1, -1):
                value = held[z] + (face[z] * value) * inv[z]
                o_ref[z, rows, :] = value
            return c

        lax.fori_loop(0, CY // 8, solve_rows, 0)

    def send_block_halo(k):
        o_ref = BL.at[k]
        for z in range(CZ):
            HYO[k, 0, pl.ds(z, 1), :] = BL[k, z, pl.ds(CY - 1, 1), :]
            HYO[k, 1, pl.ds(z, 1), :] = BL[k, z, pl.ds(0, 1), :]
        out = [
            remote(o_ref.at[0], HZ.at[k, 1], ks.at[k, 0], kr.at[k, 0], (down, b)),
            remote(o_ref.at[CZ - 1], HZ.at[k, 0], ks.at[k, 1], kr.at[k, 1], (up, b)),
            remote(HYO.at[k, 0], HY.at[k, 0], ks.at[k, 2], kr.at[k, 2], (a, right)),
            remote(HYO.at[k, 1], HY.at[k, 1], ks.at[k, 3], kr.at[k, 3], (a, left)),
        ]
        for copy in out:
            copy.start()
        return out

    def pick(table, bins):
        rows = bins.shape[0]
        spread = jnp.broadcast_to(table, (rows, 128))
        return jnp.concatenate(
            [
                jnp.take_along_axis(spread, bins[:, 128 * i : 128 * i + 128], axis=1, mode="promise_in_bounds")
                for i in range(NX // 128)
            ],
            axis=1,
        )

    def combine(ref_at, coefs):
        value = ref_at(0)
        for i, coef in enumerate(coefs):
            value = value - coef * ref_at(i + 1)
        return value

    def total_of(acc):
        part = jnp.sum(acc, axis=0, keepdims=True)
        return jnp.sum(part, axis=1, keepdims=True)

    def direction(k, tables0, tables1, coefs, other):
        table0 = combine(lambda i: tables0[i], coefs)
        table1 = combine(lambda i: tables1[i], coefs)

        def plane(z, acc):
            rz, zs = acc
            for r in range(0, CY, 8):
                rows = pl.ds(r, 8)
                value = combine(lambda i: BL[i, z, rows, :], coefs) + pick(table0, BN[z, rows, :])
                Z[k, z + 1, pl.ds(8 + r, 8), :] = value
                res = R0[z, rows, :]
                for i, coef in enumerate(coefs):
                    res = res - coef * W[i, z, rows, :]
                rz = rz + res * value
                if k > 0:
                    image = W[k - 1, z, rows, :]
                    if k > 1:
                        image = image + other * W[0, z, rows, :]
                    zs = zs + image * value
            return rz, zs

        zero = jnp.zeros((8, NX), f32)
        rz, zs = lax.fori_loop(0, CZ, plane, (zero, zero))
        for side in range(2):
            inside = a > 0 if side == 0 else a < SLABS - 1
            for r in range(0, CY, 8):
                rows = pl.ds(r, 8)
                value = combine(lambda i: HZ[i, side, rows, :], coefs) + pick(table0, HBZ[side, rows, :])
                Z[k, (CZ + 1) * side, pl.ds(8 + r, 8), :] = jnp.where(inside, value, 0.0)
            inside = b > 0 if side == 0 else b < COLS - 1
            value = combine(lambda i: HY[i, side], coefs) + pick(table1 if side == 0 else table0, HBN[side])
            value = jnp.where(inside, value, 0.0)
            for z in range(CZ):
                Z[k, z + 1, pl.ds(7 if side == 0 else 8 + CY, 1), :] = value[z : z + 1, :]
        return total_of(rz), total_of(zs)

    def image(k):
        def plane(z, acc):
            for r in range(0, CY, 8):
                rows, mine = pl.ds(8 + r, 8), pl.ds(r, 8)
                centre = Z[k, z + 1, rows, :]
                value = (
                    CZF[z + 1, mine, :] * Z[k, z + 2, rows, :]
                    + CZF[z, mine, :] * Z[k, z, rows, :]
                    + CYP[z, mine, :] * Z[k, z + 1, pl.ds(9 + r, 8), :]
                    + CYM[z, mine, :] * Z[k, z + 1, pl.ds(7 + r, 8), :]
                    + CXP[z, mine, :] * x_plus(centre)
                    + CXM[z, mine, :] * x_minus(centre)
                )
                value = DG[z, mine, :] * centre - value
                W[k, z, mine, :] = value
                acc = acc + centre * value
            return acc

        return total_of(lax.fori_loop(0, CZ, plane, jnp.zeros((8, NX), f32)))

    def dots_row(values):
        row = jnp.zeros((1, 128), f32)
        for i, value in enumerate(values):
            row = row + jnp.where(lanes_row == 64 + i, value, 0.0)
        return row

    def dot_at(row, i):
        return jnp.sum(jnp.where(lanes_row == 64 + i, row, 0.0), axis=1, keepdims=True)

    region_sums(R0)
    pl.semaphore_wait(met.at[2], len(along_y))
    for copy in rows_out:
        copy.wait_recv()
    exchange(0, 56, jnp.zeros((1, 128), f32))
    lax.fori_loop(0, CY // 8, factor_rows, 0)
    block_solve(R0, BL.at[0])
    halos = send_block_halo(0)

    for copy in bins_out:
        copy.wait_recv()
    low, high = HBZ[0], HBZ[1]
    HBZ[0] = low + jnp.where(low < S_DEV, 84, jnp.where(low < SPAN, 16, jnp.where(low < 36, 32, -32)))
    HBZ[1] = high + jnp.where(high < S_DEV, 88, jnp.where(high < SPAN, 32, jnp.where(high < 36, -16, 32)))
    for z in range(CZ):
        HBN[0, pl.ds(z, 1), :] = HBY[0, z, pl.ds(7, 1), :]
        HBN[1, pl.ds(z, 1), :] = HBY[1, z, pl.ds(0, 1), :] + 92

    tables0, tables1, coefs = [], [], []
    beta1 = gamma = before = power = None
    coefs = []
    for k in range(3):
        t0, t1 = collect(k)
        tables0.append(t0)
        tables1.append(t1)
        if k == 1:
            power, before = dot_at(t1, 0), dot_at(t1, 1)
            alpha0 = before / power
            coefs = [alpha0]
        if k == 2:
            zw, rz, zs = (dot_at(t1, i) for i in range(3))
            beta1 = rz / before
            power, before = zw + 2.0 * beta1 * zs + beta1 * beta1 * power, rz
            alpha1 = before / power
            coefs = [alpha0 + beta1 * alpha1, alpha1]
        for copy in halos:
            copy.wait_recv()
        rz, zs = direction(k, tables0, tables1, coefs, beta1)
        zw = image(k)
        row = dots_row([zw, rz, zs])
        if k < 2:
            region_sums(W.at[k])
            exchange(k + 1, 56, row)
            block_solve(W.at[k], BL.at[k + 1])
            halos_next = send_block_halo(k + 1)
            for copy in halos:
                copy.wait_send()
            halos = halos_next
    for copy in halos:
        copy.wait_send()

    M3[...] = row

    everyone(lambda device: remote(M3, G3.at[me], gs.at[3], gr.at[3], device).start())
    G3[me] = M3[...]
    for copy in halo + bins_out + rows_out:
        copy.wait_send()
    for k in range(3):
        part = M.at[k, pl.ds(0, DEVS - 1)]
        pltpu.make_async_copy(part, part, gs.at[k]).wait()
    part = G3.at[pl.ds(0, DEVS - 1)]
    pltpu.make_async_copy(part, part, gr.at[3]).wait()

    def add(i, acc):
        return acc + G3[pl.ds(8 * i, 8)]

    total = jnp.sum(lax.fori_loop(0, DEVS // 8, add, jnp.zeros((8, 1, 128), f32)), axis=0)
    zw, rz, zs = (dot_at(total, i) for i in range(3))
    beta2 = rz / before
    power = zw + 2.0 * beta2 * zs + beta2 * beta2 * power
    alpha2 = rz / power
    c1 = alpha1 + beta2 * alpha2
    c0 = alpha0 + beta1 * c1

    def finish(z, c):
        for r in range(0, CY, 8):
            rows, inner = pl.ds(r, 8), pl.ds(8 + r, 8)
            out_x[z, rows, :] = c0 * Z[0, z + 1, inner, :] + c1 * Z[1, z + 1, inner, :] + alpha2 * Z[2, z + 1, inner, :]
            out_r[z, rows, :] = R0[z, rows, :] - (
                c0 * W[0, z, rows, :] + c1 * W[1, z, rows, :] + alpha2 * W[2, z, rows, :]
            )
        return c

    lax.fori_loop(0, CZ, finish, 0)
    pltpu.make_async_copy(part, part, gs.at[3]).wait()


def on_device(fraction, source, bubble_label, subdomain, coarse_inverse):
    out = jax.ShapeDtypeStruct(fraction.shape, f32)
    hbm = pl.BlockSpec(memory_space=pl.ANY)
    vmem = pl.BlockSpec(memory_space=pltpu.VMEM)
    block = (CZ, CY, NX)

    def buf(*shape, dtype=f32):
        return pltpu.VMEM(shape, dtype)

    dma = pltpu.SemaphoreType.DMA
    return pl.pallas_call(
        kernel,
        out_shape=(out, out),
        in_specs=[hbm] * 5,
        out_specs=(vmem, vmem),
        scratch_shapes=[
            buf(CZ + 6, 64, NX),
            buf(4, 4, NX),
            buf(4, 4, NX),
            buf(3, CZ + 4, 64, NX),
            buf(CZ + 2, 64, NX),
            buf(*block),
            buf(*block, dtype=jnp.int32),
            buf(*block, dtype=jnp.int32),
            buf(*block, dtype=jnp.int32),
            buf(SPAN, DEVS * SPAN),
            buf(56, DEVS * SPAN),
            buf(CZ + 1, CY, NX),
            buf(*block),
            buf(*block),
            buf(*block),
            buf(*block),
            buf(*block),
            buf(*block),
            buf(*block),
            buf(3, *block),
            buf(3, *block),
            buf(3, CZ + 2, 48, NX),
            buf(2, CY, NX, dtype=jnp.int32),
            buf(2, CZ, 8, NX, dtype=jnp.int32),
            buf(3, 2, CY, NX),
            buf(3, 2, CZ, NX),
            buf(2, CZ, NX, dtype=jnp.int32),
            buf(3, 2, CZ, NX),
            buf(56, 128),
            buf(48, 256),
            buf(COLS, 48, 128),
            buf(COLS, 48, 128),
            buf(3, DEVS, 2, 128),
            buf(3, DEVS, 2, 128),
            buf(1, 128),
            buf(DEVS, 1, 128),
            dma((5,)),
            dma((8,)),
            dma((8,)),
            dma((4,)),
            dma((4,)),
            dma((2,)),
            dma((2,)),
            dma((3, 4)),
            dma((3, 4)),
            dma((4,)),
            dma((4,)),
            pltpu.SemaphoreType.REGULAR((3,)),
        ],
        compiler_params=pltpu.CompilerParams(
            collective_id=0, has_side_effects=True, vmem_limit_bytes=56 * 2**20
        ),
    )(fraction, source, bubble_label, subdomain, coarse_inverse)


def solution(mesh):
    placed = (P("gz", "gy", None),) * 4 + (P(("gz", "gy"), None),)
    return jax.shard_map(
        on_device, mesh=mesh, in_specs=placed, out_specs=(P("gz", "gy", None),) * 2, check_vma=False
    )
```
